32 devices in a mesh: ty: 4 (over y, core), tx: 8 (over z, x).
Axes of the slice: x: 2, y: 2, z: 4, core: 2. Of those that a mesh axis runs over, the one named last changes fastest.
Arguments:
- section_a: bfloat16 [2048, 4096], P('ty', 'tx'), may hold values from -6 to 6
- section_b: bfloat16 [2048, 4096], P('ty', 'tx'), may hold values from -6 to 6
- template_corner: int32 [2, 4, 64], P(None, 'ty', 'tx'), may hold values from 0 to 384
- template_slot: int32 [4, 64], P('ty', 'tx'), may hold values from 0 to 15, as said below
- window_corner: int32 [2, 4, 64], P(None, 'ty', 'tx'), may hold values from 0 to 384
- window_slot: int32 [4, 64], P('ty', 'tx'), may hold values from 0 to 15, as said below
- node_mask: int32 [128, 256], P('ty', 'tx'), may hold values 0 or 1
Outputs:
- owner_flow: float32 [2, 4, 64], P(None, 'ty', 'tx')
- source_flow: float32 [2, 4, 64], P(None, 'ty', 'tx')
- displacement: float32 [2, 128, 256], P(None, 'ty', 'tx')
The draws below stay inside these ranges and needn't reach their ends.
Inputs may be any that keep to these rules, and one draw needn't show every extreme that they name: `template_slot`: entry j of a row belongs to owner device j // 8 of that ty row; its value is s * 2 + k for the k-th pair that source device s sends to it; the values of one device's list are distinct; each owner gets exactly 2 pairs from each of 4 sources. `window_slot`: entry m of a row belongs to source device m // 8 of that ty row; its value is o * 2 + k for the k-th pair that it sends to owner device o; the values of one device's list are distinct; together with template_slot every pair of a row appears once on each side.
All inputs are finite; a program needn't handle non-finite values. No bound on the sum of `node_mask` on one device may be relied on, other than what follows from the above.
Results may differ from the reference program's by a relative error of at most 0.0003.
Values may be sent and summed in bfloat16 or wider, within the bound.
A program may use at most 64 MiB of HBM per device.

```python
import jax
import jax.numpy as jnp
from jax import lax

TILE = 512
PATCH = 128
SHIFTS = 65
RADIUS = 32
WIN = 192
ITEMS_DEV = 8
CAP = 2
ITEMS = 64
MY = 32
MX = 32
ITERS_R = 3
ROWS = 2048
COLS = 4096
NODE_ROWS = 128
NODE_COLS = 256
N_TY = 4
N_TX = 8


def image_draw(key):
    keys = jax.random.split(key, 3)
    image = jnp.clip(jax.random.normal(keys[2], (ROWS, COLS), jnp.float32), -6.0, 6.0)
    return image.astype(jnp.bfloat16)


def draw_section_a(key, part):
    return image_draw(jax.random.fold_in(key, 11))


def draw_section_b(key, part):
    return image_draw(jax.random.fold_in(key, 23))


def item_tables(key):
    groups = ITEMS_DEV // CAP
    span = TILE - PATCH + 1

    def arrange(values, order):
        flat = values.reshape(values.shape[:-3] + (N_TX, ITEMS_DEV))
        picked = jnp.take_along_axis(flat, jnp.broadcast_to(order, flat.shape), axis=-1)
        return picked.reshape(values.shape[:-3] + (N_TX * ITEMS_DEV,))

    def one_row(row_key):
        keys = jax.random.split(row_key, 5)
        shifts = jax.random.permutation(keys[0], N_TX)[:groups]
        sigma = jax.random.permutation(keys[1], N_TX)
        inverse = jnp.argsort(sigma)
        corners = jax.random.randint(keys[2], (4, N_TX, groups, CAP), 0, span)
        corners = corners.at[0:2, 0, 0, 0].set(jnp.array([0, span - 1], dtype=jnp.int32))
        corners = corners.at[2:4, :, 0, 0].set(span - 1)
        corners = corners.at[2:4, :, 0, CAP - 1].set(0)
        device_ids = jnp.arange(N_TX)[:, None, None]
        group_ids = jnp.broadcast_to(jnp.arange(groups)[None, :, None], (N_TX, groups, CAP))
        rank_ids = jnp.broadcast_to(jnp.arange(CAP)[None, None, :], (N_TX, groups, CAP))
        owners = jnp.broadcast_to(sigma[(device_ids + shifts[group_ids[:, :, :1]]) % N_TX], (N_TX, groups, CAP))
        send_slot = owners * CAP + rank_ids
        sources = jnp.broadcast_to((inverse[device_ids] - shifts[group_ids[:, :, :1]]) % N_TX, (N_TX, groups, CAP))
        recv_slot = sources * CAP + rank_ids
        a_corner = corners[0:2][:, sources, group_ids, rank_ids]
        b_corner = corners[2:4]
        order_a = jax.vmap(lambda sub_key: jax.random.permutation(sub_key, ITEMS_DEV))(jax.random.split(keys[3], N_TX))
        order_b = jax.vmap(lambda sub_key: jax.random.permutation(sub_key, ITEMS_DEV))(jax.random.split(keys[4], N_TX))
        return (arrange(a_corner, order_a), arrange(recv_slot, order_a), arrange(b_corner, order_b), arrange(send_slot, order_b))
    return jax.vmap(one_row)(jax.random.split(key, N_TY))


def draw_template_corner(key, part):
    tables = item_tables(jax.random.fold_in(key, 7))
    return jnp.transpose(tables[0], (1, 0, 2)).astype(jnp.int32)


def draw_template_slot(key, part):
    return item_tables(jax.random.fold_in(key, 7))[1].astype(jnp.int32)


def draw_window_corner(key, part):
    tables = item_tables(jax.random.fold_in(key, 7))
    return jnp.transpose(tables[2], (1, 0, 2)).astype(jnp.int32)


def draw_window_slot(key, part):
    return item_tables(jax.random.fold_in(key, 7))[3].astype(jnp.int32)


def touch_ends(drawn, stream_key, least, high):
    index_at = [jax.random.randint(jax.random.fold_in(stream_key, axis), (), 0, length) for axis, length in enumerate(drawn.shape)]
    main_axis = drawn.shape.index(max(drawn.shape))
    neighbour = index_at[:main_axis] + [(index_at[main_axis] + 1) % drawn.shape[main_axis]] + index_at[main_axis + 1:]
    return drawn.at[tuple(index_at)].set(least).at[tuple(neighbour)].set(high)


def setup_inputs(seed: int = 0) -> dict:
    key_of = jax.random.split(jax.random.key(seed), 8)
    return {
        "section_a": draw_section_a(jax.random.fold_in(key_of[7], 71), 0),
        "section_b": draw_section_b(jax.random.fold_in(key_of[7], 71), 0),
        "template_corner": draw_template_corner(jax.random.fold_in(key_of[7], 71), 0),
        "template_slot": draw_template_slot(jax.random.fold_in(key_of[7], 71), 0),
        "window_corner": draw_window_corner(jax.random.fold_in(key_of[7], 71), 0),
        "window_slot": draw_window_slot(jax.random.fold_in(key_of[7], 71), 0),
        "node_mask": touch_ends((jax.random.randint(key_of[6], (NODE_ROWS, NODE_COLS), 0, 8) < 7).astype(jnp.int32), jax.random.fold_in(key_of[6], 1), 0, 1),
    }


SHARPNESS = 256.0
SPRING_RATE = 0.25
FLOW_RATE = 0.5
FLOW_UNIT = 8.0
EPSILON = 1e-05

def block_flow(template, window):
    temp_f = template.astype(jnp.float32)
    wind_f = window.astype(jnp.float32)
    stacked = jnp.stack([wind_f[offset:offset + PATCH] for offset in range(SHIFTS)])
    products = jnp.einsum('ij,dik->djk', temp_f, stacked, precision=lax.Precision.HIGHEST)
    padded = jnp.pad(products, ((0, 0), (0, 0), (0, 1)))
    flat = padded.reshape(SHIFTS, PATCH * (WIN + 1))
    flat = jnp.pad(flat, ((0, 0), (0, PATCH)))
    skewed = flat.reshape(SHIFTS, PATCH, WIN + 2)[:, :, :SHIFTS]
    corr = lax.optimization_barrier(jnp.sum(skewed, axis=1))
    energy_t = jnp.mean(temp_f * temp_f)
    energy_w = jnp.mean(wind_f * wind_f)
    scores = SHARPNESS * corr / (PATCH * PATCH * jnp.sqrt((energy_t + EPSILON) * (energy_w + EPSILON)))
    weights = jnp.exp(scores - jnp.max(scores))
    weights = weights / jnp.sum(weights)
    shift_vals = (jnp.arange(SHIFTS) - RADIUS).astype(jnp.float32)
    flow_y = jnp.sum(weights * shift_vals[:, None]) / FLOW_UNIT
    flow_x = jnp.sum(weights * shift_vals[None, :]) / FLOW_UNIT
    return jnp.stack([flow_y, flow_x])

def relax_sweep(padded, mask_pad, target, count):
    centre = padded[:, 1:-1, 1:-1]
    mask_c = mask_pad[1:-1, 1:-1]
    height = centre.shape[1]
    width = centre.shape[2]
    spring = jnp.zeros_like(centre)
    for row_step, col_step in ((0, 1), (2, 1), (1, 0), (1, 2)):
        nearby = padded[:, row_step:row_step + height, col_step:col_step + width]
        mask_n = mask_pad[row_step:row_step + height, col_step:col_step + width]
        spring = spring + mask_c * mask_n * (nearby - centre)
    return centre + SPRING_RATE * spring + FLOW_RATE * (target - count * centre)

def reference(section_a, section_b, template_corner, template_slot, window_corner, window_slot, node_mask):
    slot_count = N_TX * CAP
    entry_ids = jnp.arange(ITEMS, dtype=jnp.int32)
    device_of = entry_ids // ITEMS_DEV
    row_ids = jnp.broadcast_to(jnp.arange(N_TY, dtype=jnp.int32)[:, None], (N_TY, ITEMS))
    keys_b = device_of[None, :] * slot_count + window_slot
    table = jnp.zeros((N_TY, N_TX * slot_count), jnp.int32)
    table = table.at[row_ids, keys_b].set(jnp.broadcast_to(entry_ids[None, :], (N_TY, ITEMS)))
    source_a = template_slot // CAP
    rank_a = template_slot % CAP
    keys_a = source_a * slot_count + device_of[None, :] * CAP + rank_a
    partner = jnp.take_along_axis(table, keys_a, axis=1).astype(jnp.int32)
    padded_b = jnp.pad(section_b, RADIUS)
    a_top = row_ids * TILE + template_corner[0]
    a_left = device_of[None, :] * TILE + template_corner[1]
    b_top = row_ids * TILE + jnp.take_along_axis(window_corner[0], partner, axis=1)
    b_left = source_a * TILE + jnp.take_along_axis(window_corner[1], partner, axis=1)
    corners = jnp.stack([a_top.reshape(-1), a_left.reshape(-1), b_top.reshape(-1), b_left.reshape(-1)], axis=1).astype(jnp.int32)

    def one_pair(corner):
        template = lax.dynamic_slice(section_a, (corner[0], corner[1]), (PATCH, PATCH))
        window = lax.dynamic_slice(padded_b, (corner[2], corner[3]), (WIN, WIN))
        return block_flow(template, window)
    flows = lax.map(one_pair, corners)
    owner_flow = flows.T.reshape(2, N_TY, ITEMS)
    source_flow = jnp.zeros((2, N_TY, ITEMS), jnp.float32).at[:, row_ids, partner].set(-owner_flow)
    node_y = row_ids * MY + (window_corner[0] + PATCH // 2) * MY // TILE
    node_x = device_of[None, :] * MX + (window_corner[1] + PATCH // 2) * MX // TILE
    target = jnp.zeros((2, NODE_ROWS, NODE_COLS), jnp.float32).at[:, node_y, node_x].add(source_flow)
    count = jnp.zeros((NODE_ROWS, NODE_COLS), jnp.float32).at[node_y, node_x].add(jnp.ones((N_TY, ITEMS), jnp.float32))
    mask_pad = jnp.pad(node_mask.astype(jnp.float32), 1)
    displace = jnp.zeros((2, NODE_ROWS, NODE_COLS), jnp.float32)
    for sweep in range(ITERS_R):
        displace = relax_sweep(jnp.pad(displace, ((0, 0), (1, 1), (1, 1))), mask_pad, target, count)
    return (owner_flow, source_flow, displace)
```

```python
import functools

import jax
import jax.numpy as jnp
from jax import lax
from jax.experimental import pallas as pl
from jax.experimental.pallas import tpu as pltpu
from jax.sharding import PartitionSpec as P

PATCH = 128
SHIFTS = 65
RADIUS = 32
WIN = 192
CAP = 2
ITERS_R = 3
LANES = 128
GROUP = 4
SPAN = 80


SHARPNESS = 256.0
SPRING_RATE = 0.25
FLOW_RATE = 0.5
FLOW_UNIT = 8.0
EPSILON = 1e-05
VMEM = pl.BlockSpec(memory_space=pltpu.VMEM)
SMEM = pl.BlockSpec(memory_space=pltpu.SMEM)
ANY = pl.BlockSpec(memory_space=pl.ANY)


def padded_2(cells, sides, width):
    for axis, dim in sides:
        count = lax.axis_size(axis)
        ends = count - 1
        head = lax.slice_in_dim(cells, 0, width, axis=dim)
        tail = lax.slice_in_dim(cells, cells.shape[dim] - width, cells.shape[dim], axis=dim)
        cells = jnp.concatenate(
            [
                lax.ppermute(tail, axis, [(i, (i + 1) % count) for i in range(ends)]),
                cells,
                lax.ppermute(head, axis, [((i + 1) % count, i) for i in range(ends)]),
            ],
            axis=dim,
        )
    return cells


def cut_kernel(items, corner_ref, slot_ref, a_ref, out_ref, wide):
    rows, cols = a_ref.shape
    for part in range(cols // LANES):
        wide[part] = a_ref[:, part * LANES : (part + 1) * LANES].astype(jnp.float32)
    wide[cols // LANES] = jnp.zeros((rows, LANES), jnp.float32)

    def one(j, carry):
        top = corner_ref[0, 0, j]
        left = corner_ref[1, 0, j]
        base = left // LANES
        block = jnp.concatenate([wide[base + p, pl.ds(top, PATCH), :] for p in range(2)], axis=1)
        block = pltpu.roll(block, (2 * LANES - left % LANES) % (2 * LANES), 1)
        out_ref[slot_ref[0, j]] = block[:, :PATCH].astype(jnp.bfloat16)
        return carry

    lax.fori_loop(0, items, one, 0)


def cut_templates(section_a, template_corner, template_slot, slots):
    rows, cols = section_a.shape
    return pl.pallas_call(
        functools.partial(cut_kernel, template_slot.shape[1]),
        out_shape=jax.ShapeDtypeStruct((slots, PATCH, PATCH), jnp.bfloat16),
        in_specs=[SMEM, SMEM, VMEM],
        out_specs=VMEM,
        scratch_shapes=[pltpu.VMEM((cols // LANES + 1, rows, LANES), jnp.float32)],
        compiler_params=pltpu.CompilerParams(vmem_limit_bytes=24 * 2**20),
        name="cut",
    )(template_corner, template_slot, section_a)


def flow_kernel(
    items,
    left_pad,
    tile,
    corner_ref,
    slot_ref,
    b_ref,
    t_ref,
    mask_ref,
    ret_ref,
    field_ref,
    source_ref,
    wide,
    win,
    shifted,
    temp,
    corrs,
    scales,
):
    f32 = jnp.float32
    rows_b, cols_b = b_ref.shape
    for part in range(wide.shape[0]):
        held = max(0, min(LANES, cols_b - part * LANES))
        if held < LANES:
            wide[part] = jnp.zeros((rows_b, LANES), f32)
        if held:
            wide[part, :, :held] = b_ref[:, part * LANES : part * LANES + held].astype(f32)
    win[WIN:, :] = jnp.zeros((win.shape[0] - WIN, 2 * LANES), f32)
    lane = lax.broadcasted_iota(jnp.int32, (64, LANES), 1)
    shift = lax.broadcasted_iota(jnp.int32, (64, LANES), 0)
    low = (lane >= shift).astype(f32).astype(jnp.bfloat16)
    high = (lane < shift).astype(f32).astype(jnp.bfloat16)
    row_of = lax.broadcasted_iota(jnp.int32, (8, 2 * LANES), 0)
    win_lane = lax.broadcasted_iota(jnp.int32, (WIN, 2 * LANES), 1)

    def one(m, carry):
        top = corner_ref[0, 0, m]
        left = corner_ref[1, 0, m] + left_pad
        base = left // LANES
        block = jnp.concatenate([wide[base + p, pl.ds(top, WIN), :] for p in range(3)], axis=1)
        block = pltpu.roll(block, (3 * LANES - left % LANES) % (3 * LANES), 1)
        window = jnp.where(win_lane < WIN, block[:, : 2 * LANES], 0.0)
        win[:WIN, :] = window
        template = t_ref[slot_ref[0, m]]
        temp[...] = template.astype(f32)
        for s in range(16 // GROUP):
            shifted[s] = win[pl.ds(s * GROUP, shifted.shape[1]), :].astype(jnp.bfloat16)
        temp_f = temp[...]
        energy_t = jnp.sum(temp_f * temp_f, keepdims=True) / (PATCH * PATCH)
        energy_w = jnp.sum(window * window, keepdims=True) / (WIN * WIN)
        scales[m] = jnp.broadcast_to((energy_t + EPSILON) * (energy_w + EPSILON), (8, LANES))

        def rows16(step, total):
            row0 = pl.multiple_of(step * 16, 16)
            sixteen = temp[pl.ds(row0, 16), :]
            for s in range(16 // GROUP):
                parts = []
                for g in range(GROUP):
                    row = jnp.broadcast_to(
                        sixteen[s * GROUP + g : s * GROUP + g + 1, :], (64, LANES)
                    )
                    turned = pltpu.roll(row, 0, 1, stride=1, stride_axis=0)
                    turned = turned.astype(jnp.bfloat16)
                    parts.append(jnp.concatenate([turned * low, turned * high], axis=1))
                placed = jnp.concatenate(parts, axis=0)
                moved = shifted[s, pl.ds(row0, SPAN), :]
                total = total + lax.dot_general(
                    moved, placed, (((1,), (1,)), ((), ())), preferred_element_type=f32
                )
            return total

        total = lax.fori_loop(
            0, PATCH // 16, rows16, jnp.zeros((SPAN, GROUP * 64), f32)
        )
        corr = total[:, :64]
        for g in range(1, GROUP):
            part = pltpu.roll(total, SPAN - g, 0)
            corr = corr + part[:, g * 64 : g * 64 + 64]
        corrs[m, :72, :64] = corr[:72]
        far = pltpu.roll(window, 2 * LANES - 64, 1)[:, :LANES].astype(jnp.bfloat16)
        far = jnp.concatenate([far, jnp.zeros((2 * LANES - WIN, LANES), jnp.bfloat16)], axis=0)
        cross = lax.dot_general(
            template, far, (((1,), (1,)), ((), ())), preferred_element_type=f32
        )
        moved = cross[:8]
        for q in range(1, PATCH // 8):
            moved = moved + pltpu.roll(cross[8 * q : 8 * q + 8], 2 * LANES - 8 * q, 1)
        for bit in (1, 2, 4):
            moved = jnp.where(row_of & bit != 0, pltpu.roll(moved, 2 * LANES - bit, 1), moved)
        last = jnp.sum(moved, axis=0, keepdims=True)
        corrs[m, 72:80, :] = jnp.broadcast_to(last[:, :LANES], (8, LANES))
        return carry

    lax.fori_loop(0, items, one, 0)

    corr = corrs[:, :72, :]
    scale = SHARPNESS / (PATCH * PATCH * jnp.sqrt(scales[...]))
    scale = scale[:, 0:1, :]
    dy = lax.broadcasted_iota(jnp.int32, corr.shape, 1)
    dx = lax.broadcasted_iota(jnp.int32, corr.shape, 2)
    edge = corrs[:, 72:80, :]
    edge_at = lax.broadcasted_iota(jnp.int32, edge.shape, 2)
    edge_row = lax.broadcasted_iota(jnp.int32, edge.shape, 1)
    inside = (dy < SHIFTS) & (dx < 64)
    edge_in = (edge_at < SHIFTS) & (edge_row == 0)
    least = jnp.finfo(f32).min
    scores = jnp.where(inside, corr * scale, least)
    edges = jnp.where(edge_in, edge * scale, least)
    peak = jnp.maximum(
        jnp.max(jnp.max(scores, axis=1, keepdims=True), axis=2, keepdims=True),
        jnp.max(jnp.max(edges, axis=1, keepdims=True), axis=2, keepdims=True),
    )
    weights = jnp.where(inside, jnp.exp(scores - peak), 0.0)
    edge_w = jnp.where(edge_in, jnp.exp(edges - peak), 0.0)

    def total_of(main, rim):
        return jnp.sum(jnp.sum(main, axis=1, keepdims=True), axis=2, keepdims=True) + jnp.sum(
            jnp.sum(rim, axis=1, keepdims=True), axis=2, keepdims=True
        )

    norm = total_of(weights, edge_w)
    flow_y = (
        total_of(weights * (dy - RADIUS).astype(f32), edge_w * (edge_at - RADIUS).astype(f32))
        / norm
        / FLOW_UNIT
    )
    flow_x = (
        total_of(weights * (dx - RADIUS).astype(f32), edge_w * float(64 - RADIUS))
        / norm
        / FLOW_UNIT
    )
    flow_y = jnp.broadcast_to(flow_y, (items, 1, LANES))
    flow_x = jnp.broadcast_to(flow_x, (items, 1, LANES))
    node_rows, node_cols = mask_ref.shape
    at_row = lax.broadcasted_iota(jnp.int32, (node_rows, LANES), 0)
    at_col = lax.broadcasted_iota(jnp.int32, (node_rows, LANES), 1)
    target_y = jnp.zeros((node_rows, LANES), f32)
    target_x = jnp.zeros((node_rows, LANES), f32)
    count = jnp.zeros((node_rows, LANES), f32)
    out_lane = lax.broadcasted_iota(jnp.int32, (1, LANES), 1)
    out_y = jnp.zeros((1, LANES), f32)
    out_x = jnp.zeros((1, LANES), f32)
    for m in range(items):
        slot = slot_ref[0, m]
        ret_ref[slot // CAP, pl.ds(slot % CAP * 2, 1), :] = flow_y[m]
        ret_ref[slot // CAP, pl.ds(slot % CAP * 2 + 1, 1), :] = flow_x[m]
        centre_y = (corner_ref[0, 0, m] + PATCH // 2) * node_rows // tile
        centre_x = (corner_ref[1, 0, m] + PATCH // 2) * node_cols // tile
        here = (at_row == centre_y) & (at_col == centre_x)
        target_y = target_y - jnp.where(here, flow_y[m], 0.0)
        target_x = target_x - jnp.where(here, flow_x[m], 0.0)
        count = count + jnp.where(here, 1.0, 0.0)
        out_y = jnp.where(out_lane == m, -flow_y[m], out_y)
        out_x = jnp.where(out_lane == m, -flow_x[m], out_x)
    field_ref[...] = jnp.zeros(field_ref.shape, f32)
    field_ref[0, :, :node_cols] = mask_ref[...].astype(f32)
    field_ref[1] = target_y
    field_ref[2] = target_x
    field_ref[3] = count
    source_ref[0] = out_y[:, :items]
    source_ref[1] = out_x[:, :items]


def pair_flows(wide_b, arrived, window_corner, window_slot, node_mask, left_pad, tile, devices):
    items = window_slot.shape[1]
    rows_b = wide_b.shape[0]
    node_rows = node_mask.shape[0]
    f32 = jnp.float32
    cols_w = max(wide_b.shape[1], (tile - PATCH + left_pad) // LANES * LANES + 3 * LANES)
    cols_w = (cols_w + LANES - 1) // LANES * LANES
    return pl.pallas_call(
        functools.partial(flow_kernel, items, left_pad, tile),
        out_shape=[
            jax.ShapeDtypeStruct((devices, 8, LANES), f32),
            jax.ShapeDtypeStruct((4, node_rows, LANES), f32),
            jax.ShapeDtypeStruct((2, 1, items), f32),
        ],
        in_specs=[SMEM, SMEM, VMEM, VMEM, VMEM],
        out_specs=[VMEM, VMEM, VMEM],
        scratch_shapes=[
            pltpu.VMEM((cols_w // LANES, rows_b, LANES), f32),
            pltpu.VMEM((WIN + 32, 2 * LANES), f32),
            pltpu.VMEM((16 // GROUP, WIN + 16, 2 * LANES), jnp.bfloat16),
            pltpu.VMEM((PATCH, LANES), f32),
            pltpu.VMEM((items, 80, LANES), f32),
            pltpu.VMEM((items, 8, LANES), f32),
        ],
        compiler_params=pltpu.CompilerParams(vmem_limit_bytes=32 * 2**20),
        name="pair_flows",
    )(window_corner, window_slot, wide_b, arrived, node_mask)


def relax_sweep(padded, mask_pad, target, count):
    centre = padded[:, 1:-1, 1:-1]
    mask_c = mask_pad[1:-1, 1:-1]
    height = centre.shape[1]
    width = centre.shape[2]
    spring = jnp.zeros_like(centre)
    for row_step, col_step in ((0, 1), (2, 1), (1, 0), (1, 2)):
        nearby = padded[:, row_step : row_step + height, col_step : col_step + width]
        mask_n = mask_pad[row_step : row_step + height, col_step : col_step + width]
        spring = spring + mask_c * mask_n * (nearby - centre)
    return centre + SPRING_RATE * spring + FLOW_RATE * (target - count * centre)


def shards(
    section_a, section_b, template_corner, template_slot, window_corner, window_slot, node_mask
):
    tile = section_a.shape[0]
    devices = lax.axis_size("tx")
    slots = devices * CAP
    outgoing = cut_templates(section_a, template_corner, template_slot, slots)
    arrived = lax.all_to_all(outgoing, "tx", split_axis=0, concat_axis=0, tiled=True)
    b_wide = padded_2(section_b, (("ty", 0), ("tx", 1)), RADIUS)
    returned, stacked, source_flow = pair_flows(
        b_wide, arrived, window_corner, window_slot, node_mask, 0, tile, devices
    )
    landed = lax.all_to_all(returned, "tx", split_axis=0, concat_axis=0, tiled=True)
    by_slot = landed[:, : 2 * CAP, 0].reshape(slots, 2)
    owner_flow = jnp.sum(
        jnp.where(
            template_slot[0][None, :, None] == jnp.arange(slots, dtype=jnp.int32)[:, None, None],
            by_slot[:, None, :],
            0.0,
        ),
        axis=0,
    ).T[:, None, :]
    node_rows, node_cols = node_mask.shape
    wide = padded_2(stacked[:, :, :node_cols], (("ty", 1), ("tx", 2)), ITERS_R)
    wide_mask = jnp.pad(wide[0], 1)
    displace = jnp.zeros((2,) + wide.shape[1:], jnp.float32)
    for sweep in range(ITERS_R):
        displace = relax_sweep(
            jnp.pad(displace, ((0, 0), (1, 1), (1, 1))), wide_mask, wide[1:3], wide[3]
        )
    displace = displace[:, ITERS_R : ITERS_R + node_rows, ITERS_R : ITERS_R + node_cols]
    return (owner_flow, source_flow, displace)


def solution(mesh):
    placed = (
        P("ty", "tx"),
        P("ty", "tx"),
        P(None, "ty", "tx"),
        P("ty", "tx"),
        P(None, "ty", "tx"),
        P("ty", "tx"),
        P("ty", "tx"),
    )
    return jax.shard_map(
        shards,
        mesh=mesh,
        in_specs=placed,
        out_specs=(P(None, "ty", "tx"), P(None, "ty", "tx"), P(None, "ty", "tx")),
        check_vma=False,
    )
```

```python
import functools

import jax
import jax.numpy as jnp
from jax import lax
from jax.experimental import pallas as pl
from jax.experimental.pallas import tpu as pltpu
from jax.sharding import PartitionSpec as P

PATCH = 128
SHIFTS = 65
RADIUS = 32
WIN = 192
CAP = 2
ITERS_R = 3
LANES = 128
GROUP = 4
SPAN = 80


SHARPNESS = 256.0
SPRING_RATE = 0.25
FLOW_RATE = 0.5
FLOW_UNIT = 8.0
EPSILON = 1e-05
VMEM = pl.BlockSpec(memory_space=pltpu.VMEM)
SMEM = pl.BlockSpec(memory_space=pltpu.SMEM)
ANY = pl.BlockSpec(memory_space=pl.ANY)


DIRECTIONS = tuple((r, c) for r in (-1, 0, 1) for c in (-1, 0, 1) if (r, c) != (0, 0))
MESH = pl.DeviceIdType.MESH


def within(n_ty, n_tx, row, col):
    return (row >= 0) & (row < n_ty) & (col >= 0) & (col < n_tx)


def greet(n_ty, n_tx):
    ty, tx = lax.axis_index("ty"), lax.axis_index("tx")
    barrier = pltpu.get_barrier_semaphore()
    waits = n_tx - 1
    for step in range(1, n_tx):
        pl.semaphore_signal(
            barrier, inc=1, device_id=(ty, lax.rem(tx + step, n_tx)), device_id_type=MESH
        )
    for r, c in DIRECTIONS:
        if r == 0:
            continue
        there = within(n_ty, n_tx, ty + r, tx + c)

        @pl.when(there)
        def _():
            pl.semaphore_signal(barrier, inc=1, device_id=(ty + r, tx + c), device_id_type=MESH)

        waits = waits + there.astype(jnp.int32)
    pl.semaphore_wait(barrier, waits)


def to_row(n_tx, source, landing, width, send, recv):
    ty, tx = lax.axis_index("ty"), lax.axis_index("tx")
    copies = []
    for step in range(1, n_tx):
        peer = lax.rem(tx + step, n_tx)
        copies.append(
            pltpu.make_async_remote_copy(
                src_ref=source.at[pl.ds(peer * width, width)],
                dst_ref=landing.at[pl.ds(tx * width, width)],
                send_sem=send.at[step],
                recv_sem=recv.at[step],
                device_id=(ty, peer),
                device_id_type=MESH,
            )
        )
    return copies


def edges_of(step, size, rim, pad):
    if step == 0:
        return pl.ds(0, size), pl.ds(pad, size)
    if step < 0:
        return pl.ds(0, rim), pl.ds(pad + size, rim)
    return pl.ds(size - rim, rim), pl.ds(pad - rim, rim)


def gather_kernel(n_ty, n_tx, b_ref, out_ref, wide, landed, zeros, send, recv, hsend, hrecv, own):
    ty, tx = lax.axis_index("ty"), lax.axis_index("tx")
    rows, cols = b_ref.shape
    zeros[...] = jnp.zeros(zeros.shape, zeros.dtype)
    tile_copy = pltpu.make_async_copy(
        b_ref, wide.at[pl.ds(RADIUS, rows), pl.ds(LANES, cols)], own.at[8]
    )
    tile_copy.start()
    mine = pl.ds(tx * CAP, CAP)
    own_copy = pltpu.make_async_copy(out_ref.at[mine], landed.at[mine], own.at[9])
    own_copy.start()
    greet(n_ty, n_tx)
    copies = to_row(n_tx, out_ref, landed, CAP, send, recv)
    for copy in copies:
        copy.start()
    rims = []
    for d, (r, c) in enumerate(DIRECTIONS):
        row_from, row_to = edges_of(r, rows, RADIUS, RADIUS)
        col_from, col_to = edges_of(c, cols, LANES, LANES)
        rim = pltpu.make_async_remote_copy(
            src_ref=b_ref.at[row_from, col_from],
            dst_ref=wide.at[row_to, col_to],
            send_sem=hsend.at[d],
            recv_sem=hrecv.at[d],
            device_id=(ty + r, tx + c),
            device_id_type=MESH,
        )
        fill = pltpu.make_async_copy(
            zeros.at[pl.ds(0, row_to.size), pl.ds(0, col_to.size)],
            wide.at[row_to, col_to],
            own.at[d],
        )
        goes = within(n_ty, n_tx, ty + r, tx + c)
        comes = within(n_ty, n_tx, ty - r, tx - c)
        pl.when(goes)(rim.start)
        pl.when(jnp.logical_not(comes))(fill.start)
        rims.append((goes, comes, rim, fill))
    for goes, comes, rim, fill in rims:
        pl.when(comes)(rim.wait_recv)
        pl.when(jnp.logical_not(comes))(fill.wait)
        pl.when(goes)(rim.wait_send)
    tile_copy.wait()
    own_copy.wait()
    for copy in copies:
        copy.wait()


def gather(section_b, outgoing, n_ty, n_tx):
    rows, cols = section_b.shape
    dma = pltpu.SemaphoreType.DMA
    return pl.pallas_call(
        functools.partial(gather_kernel, n_ty, n_tx),
        out_shape=[
            jax.ShapeDtypeStruct((rows + 2 * RADIUS, cols + 2 * LANES), jnp.bfloat16),
            jax.ShapeDtypeStruct(outgoing.shape, jnp.bfloat16),
        ],
        in_specs=[ANY, ANY],
        out_specs=[ANY, ANY],
        scratch_shapes=[
            pltpu.VMEM((rows, cols), jnp.bfloat16),
            dma((n_tx,)),
            dma((n_tx,)),
            dma((8,)),
            dma((8,)),
            dma((10,)),
        ],
        compiler_params=pltpu.CompilerParams(collective_id=0, has_side_effects=True),
        name="gather",
    )(section_b, outgoing)


def relax_kernel(
    n_ty, n_tx, slot_ref, ret_ref, field_ref, owner_ref, moved_ref, landed, ext, send, recv, hsend, hrecv
):
    f32 = jnp.float32
    ty, tx = lax.axis_index("ty"), lax.axis_index("tx")
    rows = field_ref.shape[0]
    cols = moved_ref.shape[2]
    items = owner_ref.shape[2]
    greet(n_ty, n_tx)
    copies = to_row(n_tx, ret_ref, landed, 1, send, recv)
    rims = []
    for d, (r, c) in enumerate(DIRECTIONS):
        row_from, row_to = edges_of(r, rows, 8, 8)
        rim = pltpu.make_async_remote_copy(
            src_ref=field_ref.at[row_from],
            dst_ref=ext.at[1 - c, row_to],
            send_sem=hsend.at[d],
            recv_sem=hrecv.at[d],
            device_id=(ty + r, tx + c),
            device_id_type=MESH,
        )
        goes = within(n_ty, n_tx, ty + r, tx + c)
        comes = within(n_ty, n_tx, ty - r, tx - c)
        pl.when(goes)(rim.start)
        rims.append((goes, comes, rim, 1 - c, row_to))
    for copy in copies:
        copy.start()
    landed[pl.ds(tx, 1)] = ret_ref[pl.ds(tx, 1)]
    ext[1, 8 : 8 + rows, :] = field_ref[...]
    for goes, comes, rim, side, row_to in rims:

        @pl.when(jnp.logical_not(comes))
        def _():
            ext[side, row_to, :] = jnp.zeros((row_to.size, LANES), f32)

    for goes, comes, rim, side, row_to in rims:
        pl.when(comes)(rim.wait_recv)
    lane = lax.broadcasted_iota(jnp.int32, (rows + 16, LANES), 1)
    left, middle, right = ext[0], ext[1], ext[2]

    def spread(field):
        at = field * cols
        wide = jnp.where(lane < 8 + cols, pltpu.roll(middle, (8 - at) % LANES, 1), 0.0)
        wide = jnp.where(lane < 8, pltpu.roll(left, (8 - at - cols) % LANES, 1), wide)
        beyond = (lane >= 8 + cols) & (lane < 16 + cols)
        return jnp.where(beyond, pltpu.roll(right, (8 + cols - at) % LANES, 1), wide)

    def around(grid):
        return (
            pltpu.roll(grid, 1, 0),
            pltpu.roll(grid, rows + 15, 0),
            pltpu.roll(grid, 1, 1),
            pltpu.roll(grid, LANES - 1, 1),
        )

    mask, count = spread(0), spread(3)
    pairs = [mask * near for near in around(mask)]
    for axis in range(2):
        target = spread(1 + axis)
        displace = jnp.zeros((rows + 16, LANES), f32)
        for sweep in range(ITERS_R):
            spring = jnp.zeros((rows + 16, LANES), f32)
            for pair, near in zip(pairs, around(displace)):
                spring = spring + pair * (near - displace)
            displace = (
                displace + SPRING_RATE * spring + FLOW_RATE * (target - count * displace)
            )
        moved_ref[axis] = pltpu.roll(displace, LANES - 8, 1)[8 : 8 + rows, :cols]
    for copy in copies:
        copy.wait()
    for goes, comes, rim, side, row_to in rims:
        pl.when(goes)(rim.wait_send)
    out_lane = lax.broadcasted_iota(jnp.int32, (1, LANES), 1)
    for axis in range(2):
        out = jnp.zeros((1, LANES), f32)
        for j in range(items):
            slot = slot_ref[0, j]
            value = landed[slot // CAP, pl.ds(slot % CAP * 2 + axis, 1), :]
            out = jnp.where(out_lane == j, value, out)
        owner_ref[axis] = out[:, :items]


def relax(template_slot, returned, field, cols, n_ty, n_tx):
    f32 = jnp.float32
    rows = field.shape[0]
    dma = pltpu.SemaphoreType.DMA
    return pl.pallas_call(
        functools.partial(relax_kernel, n_ty, n_tx),
        out_shape=[
            jax.ShapeDtypeStruct((2, 1, template_slot.shape[1]), f32),
            jax.ShapeDtypeStruct((2, rows, cols), f32),
        ],
        in_specs=[SMEM, VMEM, VMEM],
        out_specs=[VMEM, VMEM],
        scratch_shapes=[
            pltpu.VMEM(returned.shape, f32),
            pltpu.VMEM((3, rows + 16, LANES), f32),
            dma((n_tx,)),
            dma((n_tx,)),
            dma((8,)),
            dma((8,)),
        ],
        compiler_params=pltpu.CompilerParams(collective_id=1, has_side_effects=True),
        name="relax",
    )(template_slot, returned, field)


def cut_kernel(items, corner_ref, slot_ref, a_ref, out_ref, wide):
    rows, cols = a_ref.shape
    for part in range(cols // LANES):
        wide[part] = a_ref[:, part * LANES : (part + 1) * LANES].astype(jnp.float32)
    wide[cols // LANES] = jnp.zeros((rows, LANES), jnp.float32)

    def one(j, carry):
        top = corner_ref[0, 0, j]
        left = corner_ref[1, 0, j]
        base = left // LANES
        block = jnp.concatenate([wide[base + p, pl.ds(top, PATCH), :] for p in range(2)], axis=1)
        block = pltpu.roll(block, (2 * LANES - left % LANES) % (2 * LANES), 1)
        out_ref[slot_ref[0, j]] = block[:, :PATCH].astype(jnp.bfloat16)
        return carry

    lax.fori_loop(0, items, one, 0)


def cut_templates(section_a, template_corner, template_slot, slots):
    rows, cols = section_a.shape
    return pl.pallas_call(
        functools.partial(cut_kernel, template_slot.shape[1]),
        out_shape=jax.ShapeDtypeStruct((slots, PATCH, PATCH), jnp.bfloat16),
        in_specs=[SMEM, SMEM, VMEM],
        out_specs=VMEM,
        scratch_shapes=[pltpu.VMEM((cols // LANES + 1, rows, LANES), jnp.float32)],
        compiler_params=pltpu.CompilerParams(vmem_limit_bytes=24 * 2**20),
        name="cut",
    )(template_corner, template_slot, section_a)


def flow_kernel(
    items,
    left_pad,
    tile,
    corner_ref,
    slot_ref,
    b_ref,
    t_ref,
    mask_ref,
    ret_ref,
    field_ref,
    source_ref,
    wide,
    win,
    shifted,
    temp,
    corrs,
    scales,
):
    f32 = jnp.float32
    rows_b, cols_b = b_ref.shape
    for part in range(wide.shape[0]):
        held = max(0, min(LANES, cols_b - part * LANES))
        if held < LANES:
            wide[part] = jnp.zeros((rows_b, LANES), f32)
        if held:
            wide[part, :, :held] = b_ref[:, part * LANES : part * LANES + held].astype(f32)
    win[WIN:, :] = jnp.zeros((win.shape[0] - WIN, 2 * LANES), f32)
    lane = lax.broadcasted_iota(jnp.int32, (64, LANES), 1)
    shift = lax.broadcasted_iota(jnp.int32, (64, LANES), 0)
    low = (lane >= shift).astype(f32).astype(jnp.bfloat16)
    high = (lane < shift).astype(f32).astype(jnp.bfloat16)
    row_of = lax.broadcasted_iota(jnp.int32, (8, 2 * LANES), 0)
    win_lane = lax.broadcasted_iota(jnp.int32, (WIN, 2 * LANES), 1)

    def one(m, carry):
        top = corner_ref[0, 0, m]
        left = corner_ref[1, 0, m] + left_pad
        base = left // LANES
        block = jnp.concatenate([wide[base + p, pl.ds(top, WIN), :] for p in range(3)], axis=1)
        block = pltpu.roll(block, (3 * LANES - left % LANES) % (3 * LANES), 1)
        window = jnp.where(win_lane < WIN, block[:, : 2 * LANES], 0.0)
        win[:WIN, :] = window
        template = t_ref[slot_ref[0, m]]
        temp[...] = template.astype(f32)
        for s in range(16 // GROUP):
            shifted[s] = win[pl.ds(s * GROUP, shifted.shape[1]), :].astype(jnp.bfloat16)
        temp_f = temp[...]
        energy_t = jnp.sum(temp_f * temp_f, keepdims=True) / (PATCH * PATCH)
        energy_w = jnp.sum(window * window, keepdims=True) / (WIN * WIN)
        scales[m] = jnp.broadcast_to((energy_t + EPSILON) * (energy_w + EPSILON), (8, LANES))

        def rows16(step, total):
            row0 = pl.multiple_of(step * 16, 16)
            sixteen = temp[pl.ds(row0, 16), :]
            for s in range(16 // GROUP):
                parts = []
                for g in range(GROUP):
                    row = jnp.broadcast_to(
                        sixteen[s * GROUP + g : s * GROUP + g + 1, :], (64, LANES)
                    )
                    turned = pltpu.roll(row, 0, 1, stride=1, stride_axis=0)
                    turned = turned.astype(jnp.bfloat16)
                    parts.append(jnp.concatenate([turned * low, turned * high], axis=1))
                placed = jnp.concatenate(parts, axis=0)
                moved = shifted[s, pl.ds(row0, SPAN), :]
                total = total + lax.dot_general(
                    moved, placed, (((1,), (1,)), ((), ())), preferred_element_type=f32
                )
            return total

        total = lax.fori_loop(
            0, PATCH // 16, rows16, jnp.zeros((SPAN, GROUP * 64), f32)
        )
        corr = total[:, :64]
        for g in range(1, GROUP):
            part = pltpu.roll(total, SPAN - g, 0)
            corr = corr + part[:, g * 64 : g * 64 + 64]
        corrs[m, :72, :64] = corr[:72]
        far = pltpu.roll(window, 2 * LANES - 64, 1)[:, :LANES].astype(jnp.bfloat16)
        far = jnp.concatenate([far, jnp.zeros((2 * LANES - WIN, LANES), jnp.bfloat16)], axis=0)
        cross = lax.dot_general(
            template, far, (((1,), (1,)), ((), ())), preferred_element_type=f32
        )
        moved = cross[:8]
        for q in range(1, PATCH // 8):
            moved = moved + pltpu.roll(cross[8 * q : 8 * q + 8], 2 * LANES - 8 * q, 1)
        for bit in (1, 2, 4):
            moved = jnp.where(row_of & bit != 0, pltpu.roll(moved, 2 * LANES - bit, 1), moved)
        last = jnp.sum(moved, axis=0, keepdims=True)
        corrs[m, 72:80, :] = jnp.broadcast_to(last[:, :LANES], (8, LANES))
        return carry

    lax.fori_loop(0, items, one, 0)

    corr = corrs[:, :72, :]
    scale = SHARPNESS / (PATCH * PATCH * jnp.sqrt(scales[...]))
    scale = scale[:, 0:1, :]
    dy = lax.broadcasted_iota(jnp.int32, corr.shape, 1)
    dx = lax.broadcasted_iota(jnp.int32, corr.shape, 2)
    edge = corrs[:, 72:80, :]
    edge_at = lax.broadcasted_iota(jnp.int32, edge.shape, 2)
    edge_row = lax.broadcasted_iota(jnp.int32, edge.shape, 1)
    inside = (dy < SHIFTS) & (dx < 64)
    edge_in = (edge_at < SHIFTS) & (edge_row == 0)
    least = jnp.finfo(f32).min
    scores = jnp.where(inside, corr * scale, least)
    edges = jnp.where(edge_in, edge * scale, least)
    peak = jnp.maximum(
        jnp.max(jnp.max(scores, axis=1, keepdims=True), axis=2, keepdims=True),
        jnp.max(jnp.max(edges, axis=1, keepdims=True), axis=2, keepdims=True),
    )
    weights = jnp.where(inside, jnp.exp(scores - peak), 0.0)
    edge_w = jnp.where(edge_in, jnp.exp(edges - peak), 0.0)

    def total_of(main, rim):
        return jnp.sum(jnp.sum(main, axis=1, keepdims=True), axis=2, keepdims=True) + jnp.sum(
            jnp.sum(rim, axis=1, keepdims=True), axis=2, keepdims=True
        )

    norm = total_of(weights, edge_w)
    flow_y = (
        total_of(weights * (dy - RADIUS).astype(f32), edge_w * (edge_at - RADIUS).astype(f32))
        / norm
        / FLOW_UNIT
    )
    flow_x = (
        total_of(weights * (dx - RADIUS).astype(f32), edge_w * float(64 - RADIUS))
        / norm
        / FLOW_UNIT
    )
    flow_y = jnp.broadcast_to(flow_y, (items, 1, LANES))
    flow_x = jnp.broadcast_to(flow_x, (items, 1, LANES))
    node_rows, node_cols = mask_ref.shape
    at_row = lax.broadcasted_iota(jnp.int32, (node_rows, LANES), 0)
    at_col = lax.broadcasted_iota(jnp.int32, (node_rows, LANES), 1)
    field = jnp.zeros((node_rows, LANES), f32)
    out_lane = lax.broadcasted_iota(jnp.int32, (1, LANES), 1)
    out_y = jnp.zeros((1, LANES), f32)
    out_x = jnp.zeros((1, LANES), f32)
    for m in range(items):
        slot = slot_ref[0, m]
        ret_ref[slot // CAP, pl.ds(slot % CAP * 2, 1), :] = flow_y[m]
        ret_ref[slot // CAP, pl.ds(slot % CAP * 2 + 1, 1), :] = flow_x[m]
        centre_y = (corner_ref[0, 0, m] + PATCH // 2) * node_rows // tile
        centre_x = (corner_ref[1, 0, m] + PATCH // 2) * node_cols // tile
        here = at_row == centre_y
        for part, value in ((1, -flow_y[m]), (2, -flow_x[m]), (3, 1.0)):
            at = at_col == centre_x + part * node_cols
            field = field + jnp.where(here & at, value, 0.0)
        out_y = jnp.where(out_lane == m, -flow_y[m], out_y)
        out_x = jnp.where(out_lane == m, -flow_x[m], out_x)
    field_ref[...] = field
    field_ref[:, :node_cols] = mask_ref[...].astype(f32)
    source_ref[0] = out_y[:, :items]
    source_ref[1] = out_x[:, :items]


def pair_flows(wide_b, arrived, window_corner, window_slot, node_mask, left_pad, tile, devices):
    items = window_slot.shape[1]
    rows_b = wide_b.shape[0]
    node_rows = node_mask.shape[0]
    f32 = jnp.float32
    cols_w = max(wide_b.shape[1], (tile - PATCH + left_pad) // LANES * LANES + 3 * LANES)
    cols_w = (cols_w + LANES - 1) // LANES * LANES
    return pl.pallas_call(
        functools.partial(flow_kernel, items, left_pad, tile),
        out_shape=[
            jax.ShapeDtypeStruct((devices, 8, LANES), f32),
            jax.ShapeDtypeStruct((node_rows, LANES), f32),
            jax.ShapeDtypeStruct((2, 1, items), f32),
        ],
        in_specs=[SMEM, SMEM, VMEM, VMEM, VMEM],
        out_specs=[VMEM, VMEM, VMEM],
        scratch_shapes=[
            pltpu.VMEM((cols_w // LANES, rows_b, LANES), f32),
            pltpu.VMEM((WIN + 32, 2 * LANES), f32),
            pltpu.VMEM((16 // GROUP, WIN + 16, 2 * LANES), jnp.bfloat16),
            pltpu.VMEM((PATCH, LANES), f32),
            pltpu.VMEM((items, 80, LANES), f32),
            pltpu.VMEM((items, 8, LANES), f32),
        ],
        compiler_params=pltpu.CompilerParams(vmem_limit_bytes=32 * 2**20),
        name="pair_flows",
    )(window_corner, window_slot, wide_b, arrived, node_mask)


def shards(
    section_a, section_b, template_corner, template_slot, window_corner, window_slot, node_mask
):
    tile = section_a.shape[0]
    n_ty, n_tx = lax.axis_size("ty"), lax.axis_size("tx")
    outgoing = cut_templates(section_a, template_corner, template_slot, n_tx * CAP)
    b_wide, arrived = gather(section_b, outgoing, n_ty, n_tx)
    returned, field, source_flow = pair_flows(
        b_wide, arrived, window_corner, window_slot, node_mask, LANES - RADIUS, tile, n_tx
    )
    owner_flow, displace = relax(
        template_slot, returned, field, node_mask.shape[1], n_ty, n_tx
    )
    return (owner_flow, source_flow, displace)


def solution(mesh):
    placed = (
        P("ty", "tx"),
        P("ty", "tx"),
        P(None, "ty", "tx"),
        P("ty", "tx"),
        P(None, "ty", "tx"),
        P("ty", "tx"),
        P("ty", "tx"),
    )
    return jax.shard_map(
        shards,
        mesh=mesh,
        in_specs=placed,
        out_specs=(P(None, "ty", "tx"), P(None, "ty", "tx"), P(None, "ty", "tx")),
        check_vma=False,
    )
```

```python
import functools

import jax
import jax.numpy as jnp
from jax import lax
from jax.experimental import pallas as pl
from jax.experimental.pallas import tpu as pltpu
from jax.sharding import PartitionSpec as P

PATCH = 128
SHIFTS = 65
RADIUS = 32
WIN = 192
CAP = 2
ITERS_R = 3
LANES = 128
GROUP = 4
SPAN = 128


SHARPNESS = 256.0
SPRING_RATE = 0.25
FLOW_RATE = 0.5
FLOW_UNIT = 8.0
EPSILON = 1e-05
VMEM = pl.BlockSpec(memory_space=pltpu.VMEM)
SMEM = pl.BlockSpec(memory_space=pltpu.SMEM)
ANY = pl.BlockSpec(memory_space=pl.ANY)


DIRECTIONS = tuple((r, c) for r in (-1, 0, 1) for c in (-1, 0, 1) if (r, c) != (0, 0))
MESH = pl.DeviceIdType.MESH


def within(n_ty, n_tx, row, col):
    return (row >= 0) & (row < n_ty) & (col >= 0) & (col < n_tx)


def greet(n_ty, n_tx):
    ty, tx = lax.axis_index("ty"), lax.axis_index("tx")
    barrier = pltpu.get_barrier_semaphore()
    waits = n_tx - 1
    for step in range(1, n_tx):
        pl.semaphore_signal(
            barrier, inc=1, device_id=(ty, lax.rem(tx + step, n_tx)), device_id_type=MESH
        )
    for r, c in DIRECTIONS:
        if r == 0:
            continue
        there = within(n_ty, n_tx, ty + r, tx + c)

        @pl.when(there)
        def _():
            pl.semaphore_signal(barrier, inc=1, device_id=(ty + r, tx + c), device_id_type=MESH)

        waits = waits + there.astype(jnp.int32)
    pl.semaphore_wait(barrier, waits)


def to_row(n_tx, source, landing, width, send, recv):
    ty, tx = lax.axis_index("ty"), lax.axis_index("tx")
    copies = []
    for step in range(1, n_tx):
        peer = lax.rem(tx + step, n_tx)
        copies.append(
            pltpu.make_async_remote_copy(
                src_ref=source.at[pl.ds(peer * width, width)],
                dst_ref=landing.at[pl.ds(tx * width, width)],
                send_sem=send.at[step],
                recv_sem=recv.at[step],
                device_id=(ty, peer),
                device_id_type=MESH,
            )
        )
    return copies


def edges_of(step, size, rim, pad):
    if step == 0:
        return pl.ds(0, size), pl.ds(pad, size)
    if step < 0:
        return pl.ds(0, rim), pl.ds(pad + size, rim)
    return pl.ds(size - rim, rim), pl.ds(pad - rim, rim)


def gather_kernel(n_ty, n_tx, b_ref, out_ref, wide, landed, zeros, send, recv, hsend, hrecv, own):
    ty, tx = lax.axis_index("ty"), lax.axis_index("tx")
    rows, cols = b_ref.shape
    zeros[...] = jnp.zeros(zeros.shape, zeros.dtype)
    tile_copy = pltpu.make_async_copy(
        b_ref, wide.at[pl.ds(RADIUS, rows), pl.ds(LANES, cols)], own.at[8]
    )
    tile_copy.start()
    mine = pl.ds(tx * CAP, CAP)
    own_copy = pltpu.make_async_copy(out_ref.at[mine], landed.at[mine], own.at[9])
    own_copy.start()
    greet(n_ty, n_tx)
    copies = to_row(n_tx, out_ref, landed, CAP, send, recv)
    for copy in copies:
        copy.start()
    rims = []
    for d, (r, c) in enumerate(DIRECTIONS):
        row_from, row_to = edges_of(r, rows, RADIUS, RADIUS)
        col_from, col_to = edges_of(c, cols, LANES, LANES)
        rim = pltpu.make_async_remote_copy(
            src_ref=b_ref.at[row_from, col_from],
            dst_ref=wide.at[row_to, col_to],
            send_sem=hsend.at[d],
            recv_sem=hrecv.at[d],
            device_id=(ty + r, tx + c),
            device_id_type=MESH,
        )
        fill = pltpu.make_async_copy(
            zeros.at[pl.ds(0, row_to.size), pl.ds(0, col_to.size)],
            wide.at[row_to, col_to],
            own.at[d],
        )
        goes = within(n_ty, n_tx, ty + r, tx + c)
        comes = within(n_ty, n_tx, ty - r, tx - c)
        pl.when(goes)(rim.start)
        pl.when(jnp.logical_not(comes))(fill.start)
        rims.append((goes, comes, rim, fill))
    for goes, comes, rim, fill in rims:
        pl.when(comes)(rim.wait_recv)
        pl.when(jnp.logical_not(comes))(fill.wait)
        pl.when(goes)(rim.wait_send)
    tile_copy.wait()
    own_copy.wait()
    for copy in copies:
        copy.wait()


def gather(section_b, outgoing, n_ty, n_tx):
    rows, cols = section_b.shape
    dma = pltpu.SemaphoreType.DMA
    return pl.pallas_call(
        functools.partial(gather_kernel, n_ty, n_tx),
        out_shape=[
            jax.ShapeDtypeStruct((rows + 2 * RADIUS, cols + 2 * LANES), jnp.bfloat16),
            jax.ShapeDtypeStruct(outgoing.shape, jnp.bfloat16),
        ],
        in_specs=[ANY, ANY],
        out_specs=[ANY, ANY],
        scratch_shapes=[
            pltpu.VMEM((rows, cols), jnp.bfloat16),
            dma((n_tx,)),
            dma((n_tx,)),
            dma((8,)),
            dma((8,)),
            dma((10,)),
        ],
        compiler_params=pltpu.CompilerParams(
            collective_id=0, has_side_effects=True, vmem_limit_bytes=8 * 2**20
        ),
        name="gather",
    )(section_b, outgoing)


def relax_kernel(
    n_ty, n_tx, slot_ref, ret_ref, field_ref, owner_ref, moved_ref, landed, ext, send, recv, hsend, hrecv
):
    f32 = jnp.float32
    ty, tx = lax.axis_index("ty"), lax.axis_index("tx")
    rows = field_ref.shape[0]
    cols = moved_ref.shape[2]
    items = owner_ref.shape[2]
    greet(n_ty, n_tx)
    copies = to_row(n_tx, ret_ref, landed, 1, send, recv)
    rims = []
    for d, (r, c) in enumerate(DIRECTIONS):
        row_from, row_to = edges_of(r, rows, 8, 8)
        rim = pltpu.make_async_remote_copy(
            src_ref=field_ref.at[row_from],
            dst_ref=ext.at[1 - c, row_to],
            send_sem=hsend.at[d],
            recv_sem=hrecv.at[d],
            device_id=(ty + r, tx + c),
            device_id_type=MESH,
        )
        goes = within(n_ty, n_tx, ty + r, tx + c)
        comes = within(n_ty, n_tx, ty - r, tx - c)
        pl.when(goes)(rim.start)
        rims.append((goes, comes, rim, 1 - c, row_to))
    for copy in copies:
        copy.start()
    landed[pl.ds(tx, 1)] = ret_ref[pl.ds(tx, 1)]
    ext[1, 8 : 8 + rows, :] = field_ref[...]
    for goes, comes, rim, side, row_to in rims:

        @pl.when(jnp.logical_not(comes))
        def _():
            ext[side, row_to, :] = jnp.zeros((row_to.size, LANES), f32)

    for goes, comes, rim, side, row_to in rims:
        pl.when(comes)(rim.wait_recv)
    lane = lax.broadcasted_iota(jnp.int32, (rows + 16, LANES), 1)
    left, middle, right = ext[0], ext[1], ext[2]

    def spread(field):
        at = field * cols
        wide = jnp.where(lane < 8 + cols, pltpu.roll(middle, (8 - at) % LANES, 1), 0.0)
        wide = jnp.where(lane < 8, pltpu.roll(left, (8 - at - cols) % LANES, 1), wide)
        beyond = (lane >= 8 + cols) & (lane < 16 + cols)
        return jnp.where(beyond, pltpu.roll(right, (8 + cols - at) % LANES, 1), wide)

    def around(grid):
        return (
            pltpu.roll(grid, 1, 0),
            pltpu.roll(grid, rows + 15, 0),
            pltpu.roll(grid, 1, 1),
            pltpu.roll(grid, LANES - 1, 1),
        )

    mask, count = spread(0), spread(3)
    pairs = [mask * near for near in around(mask)]
    for axis in range(2):
        target = spread(1 + axis)
        displace = jnp.zeros((rows + 16, LANES), f32)
        for sweep in range(ITERS_R):
            spring = jnp.zeros((rows + 16, LANES), f32)
            for pair, near in zip(pairs, around(displace)):
                spring = spring + pair * (near - displace)
            displace = (
                displace + SPRING_RATE * spring + FLOW_RATE * (target - count * displace)
            )
        moved_ref[axis] = pltpu.roll(displace, LANES - 8, 1)[8 : 8 + rows, :cols]
    for copy in copies:
        copy.wait()
    for goes, comes, rim, side, row_to in rims:
        pl.when(goes)(rim.wait_send)
    out_lane = lax.broadcasted_iota(jnp.int32, (1, LANES), 1)
    for axis in range(2):
        out = jnp.zeros((1, LANES), f32)
        for j in range(items):
            slot = slot_ref[0, j]
            value = landed[slot // CAP, pl.ds(slot % CAP * 2 + axis, 1), :]
            out = jnp.where(out_lane == j, value, out)
        owner_ref[axis] = out[:, :items]


def relax(template_slot, returned, field, cols, n_ty, n_tx):
    f32 = jnp.float32
    rows = field.shape[0]
    dma = pltpu.SemaphoreType.DMA
    return pl.pallas_call(
        functools.partial(relax_kernel, n_ty, n_tx),
        out_shape=[
            jax.ShapeDtypeStruct((2, 1, template_slot.shape[1]), f32),
            jax.ShapeDtypeStruct((2, rows, cols), f32),
        ],
        in_specs=[SMEM, VMEM, VMEM],
        out_specs=[VMEM, VMEM],
        scratch_shapes=[
            pltpu.VMEM(returned.shape, f32),
            pltpu.VMEM((3, rows + 16, LANES), f32),
            dma((n_tx,)),
            dma((n_tx,)),
            dma((8,)),
            dma((8,)),
        ],
        compiler_params=pltpu.CompilerParams(
            collective_id=1, has_side_effects=True, vmem_limit_bytes=8 * 2**20
        ),
        name="relax",
    )(template_slot, returned, field)


def cut_kernel(items, corner_ref, slot_ref, a_ref, out_ref, wide):
    rows, cols = a_ref.shape
    for part in range(cols // LANES):
        wide[part] = a_ref[:, part * LANES : (part + 1) * LANES].astype(jnp.float32)
    wide[cols // LANES] = jnp.zeros((rows, LANES), jnp.float32)

    def one(j, carry):
        top = corner_ref[0, 0, j]
        left = corner_ref[1, 0, j]
        base = left // LANES
        block = jnp.concatenate([wide[base + p, pl.ds(top, PATCH), :] for p in range(2)], axis=1)
        block = pltpu.roll(block, (2 * LANES - left % LANES) % (2 * LANES), 1)
        out_ref[slot_ref[0, j]] = block[:, :PATCH].astype(jnp.bfloat16)
        return carry

    lax.fori_loop(0, items, one, 0)


def cut_templates(section_a, template_corner, template_slot, slots):
    rows, cols = section_a.shape
    return pl.pallas_call(
        functools.partial(cut_kernel, template_slot.shape[1]),
        out_shape=jax.ShapeDtypeStruct((slots, PATCH, PATCH), jnp.bfloat16),
        in_specs=[SMEM, SMEM, VMEM],
        out_specs=VMEM,
        scratch_shapes=[pltpu.VMEM((cols // LANES + 1, rows, LANES), jnp.float32)],
        compiler_params=pltpu.CompilerParams(vmem_limit_bytes=24 * 2**20),
        name="cut",
    )(template_corner, template_slot, section_a)


def flow_kernel(
    items,
    left_pad,
    tile,
    corner_ref,
    slot_ref,
    b_ref,
    t_ref,
    mask_ref,
    ret_ref,
    field_ref,
    source_ref,
    wide,
    win,
    shifted,
    temp,
    corrs,
    scales,
):
    f32 = jnp.float32
    rows_b, cols_b = b_ref.shape
    for part in range(wide.shape[0]):
        held = max(0, min(LANES, cols_b - part * LANES))
        if held < LANES:
            wide[part] = jnp.zeros((rows_b, LANES), f32)
        if held:
            wide[part, :, :held] = b_ref[:, part * LANES : part * LANES + held].astype(f32)
    win[:, WIN:, :] = jnp.zeros((items, win.shape[1] - WIN, 2 * LANES), f32)
    lane = lax.broadcasted_iota(jnp.int32, (64, LANES), 1)
    shift = lax.broadcasted_iota(jnp.int32, (64, LANES), 0)
    low = (lane >= shift).astype(f32).astype(jnp.bfloat16)
    high = (lane < shift).astype(f32).astype(jnp.bfloat16)
    row_of = lax.broadcasted_iota(jnp.int32, (8, 2 * LANES), 0)
    win_lane = lax.broadcasted_iota(jnp.int32, (WIN, 2 * LANES), 1)

    def one(m, carry):
        top = corner_ref[0, 0, m]
        left = corner_ref[1, 0, m] + left_pad
        base = left // LANES
        block = jnp.concatenate([wide[base + p, pl.ds(top, WIN), :] for p in range(3)], axis=1)
        block = pltpu.roll(block, (3 * LANES - left % LANES) % (3 * LANES), 1)
        window = jnp.where(win_lane < WIN, block[:, : 2 * LANES], 0.0)
        win[m, :WIN, :] = window
        template = t_ref[slot_ref[0, m]]
        temp[m] = template.astype(f32)
        for s in range(16 // GROUP):
            shifted[m, s] = win[m, pl.ds(s * GROUP, shifted.shape[2]), :].astype(jnp.bfloat16)
        temp_f = temp[m]
        energy_t = jnp.sum(temp_f * temp_f, keepdims=True) / (PATCH * PATCH)
        energy_w = jnp.sum(window * window, keepdims=True) / (WIN * WIN)
        scales[m] = jnp.broadcast_to((energy_t + EPSILON) * (energy_w + EPSILON), (8, LANES))

        def rows16(step, total):
            row0 = pl.multiple_of(step * 16, 16)
            sixteen = temp[m, pl.ds(row0, 16), :]
            placed, moved = [], []
            for s in range(16 // GROUP):
                parts = []
                for g in range(GROUP):
                    row = jnp.broadcast_to(
                        sixteen[s * GROUP + g : s * GROUP + g + 1, :], (64, LANES)
                    )
                    turned = pltpu.roll(row, 0, 1, stride=1, stride_axis=0)
                    turned = turned.astype(jnp.bfloat16)
                    parts.append(jnp.concatenate([turned * low, turned * high], axis=1))
                placed.append(jnp.concatenate(parts, axis=0))
                moved.append(shifted[m, s, pl.ds(row0, SPAN), :])
            return total + lax.dot_general(
                jnp.concatenate(placed, axis=1),
                jnp.concatenate(moved, axis=1),
                (((1,), (1,)), ((), ())),
                preferred_element_type=f32,
            )

        total = lax.fori_loop(
            0, PATCH // 16, rows16, jnp.zeros((GROUP * 64, SPAN), f32), unroll=True
        )
        corr = total[:64]
        for g in range(1, GROUP):
            corr = corr + pltpu.roll(total[g * 64 : g * 64 + 64], SPAN - g, 1)
        corrs[m, :64, :] = corr
        far = pltpu.roll(window, 2 * LANES - 64, 1)[:, :LANES].astype(jnp.bfloat16)
        far = jnp.concatenate([far, jnp.zeros((2 * LANES - WIN, LANES), jnp.bfloat16)], axis=0)
        cross = lax.dot_general(
            template, far, (((1,), (1,)), ((), ())), preferred_element_type=f32
        )
        moved = cross[:8]
        for q in range(1, PATCH // 8):
            moved = moved + pltpu.roll(cross[8 * q : 8 * q + 8], 2 * LANES - 8 * q, 1)
        for bit in (1, 2, 4):
            moved = jnp.where(row_of & bit != 0, pltpu.roll(moved, 2 * LANES - bit, 1), moved)
        last = jnp.sum(moved, axis=0, keepdims=True)
        corrs[m, 64:72, :] = jnp.broadcast_to(last[:, :LANES], (8, LANES))
        return carry

    lax.fori_loop(0, items, one, 0, unroll=4)

    corr = corrs[...]
    scale = SHARPNESS / (PATCH * PATCH * jnp.sqrt(scales[...]))
    dx = lax.broadcasted_iota(jnp.int32, corr.shape, 1)
    dy = lax.broadcasted_iota(jnp.int32, corr.shape, 2)
    inside = (dy < SHIFTS) & (dx < SHIFTS)
    scores = jnp.where(inside, corr * scale[:, 0:1, :], jnp.finfo(f32).min)
    peak = jnp.max(jnp.max(scores, axis=1, keepdims=True), axis=2, keepdims=True)
    weights = jnp.where(inside, jnp.exp(scores - peak), 0.0)
    by_col = jnp.sum(weights, axis=1, keepdims=True)
    norm = jnp.sum(by_col, axis=2, keepdims=True)
    dy_of = (dy[:, 0:1, :] - RADIUS).astype(f32)
    flow_y = jnp.sum(by_col * dy_of, axis=2, keepdims=True) / norm / FLOW_UNIT
    by_dx = jnp.sum(weights * (dx - RADIUS).astype(f32), axis=1, keepdims=True)
    flow_x = jnp.sum(by_dx, axis=2, keepdims=True) / norm / FLOW_UNIT
    flow_y = jnp.broadcast_to(flow_y, (items, 1, LANES))
    flow_x = jnp.broadcast_to(flow_x, (items, 1, LANES))
    node_rows, node_cols = mask_ref.shape
    at_row = lax.broadcasted_iota(jnp.int32, (node_rows, LANES), 0)
    at_col = lax.broadcasted_iota(jnp.int32, (node_rows, LANES), 1)
    field = jnp.zeros((node_rows, LANES), f32)
    out_lane = lax.broadcasted_iota(jnp.int32, (1, LANES), 1)
    out_y = jnp.zeros((1, LANES), f32)
    out_x = jnp.zeros((1, LANES), f32)
    for m in range(items):
        slot = slot_ref[0, m]
        ret_ref[slot // CAP, pl.ds(slot % CAP * 2, 1), :] = flow_y[m]
        ret_ref[slot // CAP, pl.ds(slot % CAP * 2 + 1, 1), :] = flow_x[m]
        centre_y = (corner_ref[0, 0, m] + PATCH // 2) * node_rows // tile
        centre_x = (corner_ref[1, 0, m] + PATCH // 2) * node_cols // tile
        here = at_row == centre_y
        for part, value in ((1, -flow_y[m]), (2, -flow_x[m]), (3, 1.0)):
            at = at_col == centre_x + part * node_cols
            field = field + jnp.where(here & at, value, 0.0)
        out_y = jnp.where(out_lane == m, -flow_y[m], out_y)
        out_x = jnp.where(out_lane == m, -flow_x[m], out_x)
    field_ref[...] = field
    field_ref[:, :node_cols] = mask_ref[...].astype(f32)
    source_ref[0] = out_y[:, :items]
    source_ref[1] = out_x[:, :items]


def pair_flows(wide_b, arrived, window_corner, window_slot, node_mask, left_pad, tile, devices):
    items = window_slot.shape[1]
    rows_b = wide_b.shape[0]
    node_rows = node_mask.shape[0]
    f32 = jnp.float32
    cols_w = max(wide_b.shape[1], (tile - PATCH + left_pad) // LANES * LANES + 3 * LANES)
    cols_w = (cols_w + LANES - 1) // LANES * LANES
    return pl.pallas_call(
        functools.partial(flow_kernel, items, left_pad, tile),
        out_shape=[
            jax.ShapeDtypeStruct((devices, 8, LANES), f32),
            jax.ShapeDtypeStruct((node_rows, LANES), f32),
            jax.ShapeDtypeStruct((2, 1, items), f32),
        ],
        in_specs=[SMEM, SMEM, VMEM, VMEM, VMEM],
        out_specs=[VMEM, VMEM, VMEM],
        scratch_shapes=[
            pltpu.VMEM((cols_w // LANES, rows_b, LANES), f32),
            pltpu.VMEM((items, WIN + 80, 2 * LANES), f32),
            pltpu.VMEM((items, 16 // GROUP, WIN + 64, 2 * LANES), jnp.bfloat16),
            pltpu.VMEM((items, PATCH, LANES), f32),
            pltpu.VMEM((items, 72, LANES), f32),
            pltpu.VMEM((items, 8, LANES), f32),
        ],
        compiler_params=pltpu.CompilerParams(vmem_limit_bytes=32 * 2**20),
        name="pair_flows",
    )(window_corner, window_slot, wide_b, arrived, node_mask)


def shards(
    section_a, section_b, template_corner, template_slot, window_corner, window_slot, node_mask
):
    tile = section_a.shape[0]
    n_ty, n_tx = lax.axis_size("ty"), lax.axis_size("tx")
    outgoing = cut_templates(section_a, template_corner, template_slot, n_tx * CAP)
    b_wide, arrived = gather(section_b, outgoing, n_ty, n_tx)
    returned, field, source_flow = pair_flows(
        b_wide, arrived, window_corner, window_slot, node_mask, LANES - RADIUS, tile, n_tx
    )
    owner_flow, displace = relax(
        template_slot, returned, field, node_mask.shape[1], n_ty, n_tx
    )
    return (owner_flow, source_flow, displace)


def solution(mesh):
    placed = (
        P("ty", "tx"),
        P("ty", "tx"),
        P(None, "ty", "tx"),
        P("ty", "tx"),
        P(None, "ty", "tx"),
        P("ty", "tx"),
        P("ty", "tx"),
    )
    return jax.shard_map(
        shards,
        mesh=mesh,
        in_specs=placed,
        out_specs=(P(None, "ty", "tx"), P(None, "ty", "tx"), P(None, "ty", "tx")),
        check_vma=False,
    )
```

```python
import functools

import jax
import jax.numpy as jnp
from jax import lax
from jax.experimental import pallas as pl
from jax.experimental.pallas import tpu as pltpu
from jax.sharding import PartitionSpec as P

PATCH = 128
SHIFTS = 65
RADIUS = 32
WIN = 192
CAP = 2
ITERS_R = 3
LANES = 128
GROUP = 4
SPAN = 128


SHARPNESS = 256.0
SPRING_RATE = 0.25
FLOW_RATE = 0.5
FLOW_UNIT = 8.0
EPSILON = 1e-05
VMEM = pl.BlockSpec(memory_space=pltpu.VMEM)
SMEM = pl.BlockSpec(memory_space=pltpu.SMEM)
ANY = pl.BlockSpec(memory_space=pl.ANY)


DIRECTIONS = tuple((r, c) for r in (-1, 0, 1) for c in (-1, 0, 1) if (r, c) != (0, 0))
MESH = pl.DeviceIdType.MESH


def within(n_ty, n_tx, row, col):
    return (row >= 0) & (row < n_ty) & (col >= 0) & (col < n_tx)


def greet(n_ty, n_tx):
    ty, tx = lax.axis_index("ty"), lax.axis_index("tx")
    barrier = pltpu.get_barrier_semaphore()
    waits = n_tx - 1
    for step in range(1, n_tx):
        pl.semaphore_signal(
            barrier, inc=1, device_id=(ty, lax.rem(tx + step, n_tx)), device_id_type=MESH
        )
    for r, c in DIRECTIONS:
        if r == 0:
            continue
        there = within(n_ty, n_tx, ty + r, tx + c)

        @pl.when(there)
        def _():
            pl.semaphore_signal(barrier, inc=1, device_id=(ty + r, tx + c), device_id_type=MESH)

        waits = waits + there.astype(jnp.int32)
    pl.semaphore_wait(barrier, waits)


def to_row(n_tx, source, landing, width, send, recv):
    ty, tx = lax.axis_index("ty"), lax.axis_index("tx")
    copies = []
    for step in range(1, n_tx):
        peer = lax.rem(tx + step, n_tx)
        copies.append(
            pltpu.make_async_remote_copy(
                src_ref=source.at[pl.ds(peer * width, width)],
                dst_ref=landing.at[pl.ds(tx * width, width)],
                send_sem=send.at[step],
                recv_sem=recv.at[step],
                device_id=(ty, peer),
                device_id_type=MESH,
            )
        )
    return copies


def edges_of(step, size, rim, pad):
    if step == 0:
        return pl.ds(0, size), pl.ds(pad, size)
    if step < 0:
        return pl.ds(0, rim), pl.ds(pad + size, rim)
    return pl.ds(size - rim, rim), pl.ds(pad - rim, rim)


def gather_kernel(n_ty, n_tx, b_ref, out_ref, wide, landed, zeros, send, recv, hsend, hrecv, own):
    ty, tx = lax.axis_index("ty"), lax.axis_index("tx")
    rows, cols = b_ref.shape
    zeros[...] = jnp.zeros(zeros.shape, zeros.dtype)
    tile_copy = pltpu.make_async_copy(
        b_ref, wide.at[pl.ds(RADIUS, rows), pl.ds(LANES, cols)], own.at[8]
    )
    tile_copy.start()
    mine = pl.ds(tx * CAP, CAP)
    own_copy = pltpu.make_async_copy(out_ref.at[mine], landed.at[mine], own.at[9])
    own_copy.start()
    greet(n_ty, n_tx)
    copies = to_row(n_tx, out_ref, landed, CAP, send, recv)
    for copy in copies:
        copy.start()
    rims = []
    for d, (r, c) in enumerate(DIRECTIONS):
        row_from, row_to = edges_of(r, rows, RADIUS, RADIUS)
        col_from, col_to = edges_of(c, cols, LANES, LANES)
        rim = pltpu.make_async_remote_copy(
            src_ref=b_ref.at[row_from, col_from],
            dst_ref=wide.at[row_to, col_to],
            send_sem=hsend.at[d],
            recv_sem=hrecv.at[d],
            device_id=(ty + r, tx + c),
            device_id_type=MESH,
        )
        fill = pltpu.make_async_copy(
            zeros.at[pl.ds(0, row_to.size), pl.ds(0, col_to.size)],
            wide.at[row_to, col_to],
            own.at[d],
        )
        goes = within(n_ty, n_tx, ty + r, tx + c)
        comes = within(n_ty, n_tx, ty - r, tx - c)
        pl.when(goes)(rim.start)
        pl.when(jnp.logical_not(comes))(fill.start)
        rims.append((goes, comes, rim, fill))
    for goes, comes, rim, fill in rims:
        pl.when(comes)(rim.wait_recv)
        pl.when(jnp.logical_not(comes))(fill.wait)
        pl.when(goes)(rim.wait_send)
    tile_copy.wait()
    own_copy.wait()
    for copy in copies:
        copy.wait()


def gather(section_b, outgoing, n_ty, n_tx):
    rows, cols = section_b.shape
    dma = pltpu.SemaphoreType.DMA
    return pl.pallas_call(
        functools.partial(gather_kernel, n_ty, n_tx),
        out_shape=[
            jax.ShapeDtypeStruct((rows + 2 * RADIUS, cols + 2 * LANES), jnp.bfloat16),
            jax.ShapeDtypeStruct(outgoing.shape, jnp.bfloat16),
        ],
        in_specs=[ANY, ANY],
        out_specs=[ANY, ANY],
        scratch_shapes=[
            pltpu.VMEM((rows, cols), jnp.bfloat16),
            dma((n_tx,)),
            dma((n_tx,)),
            dma((8,)),
            dma((8,)),
            dma((10,)),
        ],
        compiler_params=pltpu.CompilerParams(
            collective_id=0, has_side_effects=True, vmem_limit_bytes=8 * 2**20
        ),
        name="gather",
    )(section_b, outgoing)


def relax_kernel(
    n_ty, n_tx, table_ref, ret_ref, field_ref, owner_ref, moved_ref, landed, ext, send, recv, hsend, hrecv
):
    f32 = jnp.float32
    ty, tx = lax.axis_index("ty"), lax.axis_index("tx")
    rows = field_ref.shape[0]
    cols = moved_ref.shape[2]
    items = owner_ref.shape[2]
    greet(n_ty, n_tx)
    copies = to_row(n_tx, ret_ref, landed, 1, send, recv)
    rims = []
    for d, (r, c) in enumerate(DIRECTIONS):
        row_from, row_to = edges_of(r, rows, 8, 8)
        rim = pltpu.make_async_remote_copy(
            src_ref=field_ref.at[row_from],
            dst_ref=ext.at[1 - c, row_to],
            send_sem=hsend.at[d],
            recv_sem=hrecv.at[d],
            device_id=(ty + r, tx + c),
            device_id_type=MESH,
        )
        goes = within(n_ty, n_tx, ty + r, tx + c)
        comes = within(n_ty, n_tx, ty - r, tx - c)
        pl.when(goes)(rim.start)
        rims.append((goes, comes, rim, 1 - c, row_to))
    for copy in copies:
        copy.start()
    landed[pl.ds(tx, 1)] = ret_ref[pl.ds(tx, 1)]
    ext[1, 8 : 8 + rows, :] = field_ref[...]
    for goes, comes, rim, side, row_to in rims:

        @pl.when(jnp.logical_not(comes))
        def _():
            ext[side, row_to, :] = jnp.zeros((row_to.size, LANES), f32)

    for goes, comes, rim, side, row_to in rims:
        pl.when(comes)(rim.wait_recv)
    lane = lax.broadcasted_iota(jnp.int32, (rows + 16, LANES), 1)
    left, middle, right = ext[0], ext[1], ext[2]

    def spread(field):
        at = field * cols
        wide = jnp.where(lane < 8 + cols, pltpu.roll(middle, (8 - at) % LANES, 1), 0.0)
        wide = jnp.where(lane < 8, pltpu.roll(left, (8 - at - cols) % LANES, 1), wide)
        beyond = (lane >= 8 + cols) & (lane < 16 + cols)
        return jnp.where(beyond, pltpu.roll(right, (8 + cols - at) % LANES, 1), wide)

    def around(grid):
        return (
            pltpu.roll(grid, 1, 0),
            pltpu.roll(grid, rows + 15, 0),
            pltpu.roll(grid, 1, 1),
            pltpu.roll(grid, LANES - 1, 1),
        )

    mask, count = spread(0), spread(3)
    pairs = [mask * near for near in around(mask)]
    for axis in range(2):
        target = spread(1 + axis)
        displace = jnp.zeros((rows + 16, LANES), f32)
        for sweep in range(ITERS_R):
            spring = jnp.zeros((rows + 16, LANES), f32)
            for pair, near in zip(pairs, around(displace)):
                spring = spring + pair * (near - displace)
            displace = (
                displace + SPRING_RATE * spring + FLOW_RATE * (target - count * displace)
            )
        moved_ref[axis] = pltpu.roll(displace, LANES - 8, 1)[8 : 8 + rows, :cols]
    for copy in copies:
        copy.wait()
    for goes, comes, rim, side, row_to in rims:
        pl.when(goes)(rim.wait_send)
    out_lane = lax.broadcasted_iota(jnp.int32, (1, LANES), 1)
    for axis in range(2):
        out = jnp.zeros((1, LANES), f32)
        for j in range(items):
            slot = table_ref[2, j]
            value = landed[slot // CAP, pl.ds(slot % CAP * 2 + axis, 1), :]
            out = jnp.where(out_lane == j, value, out)
        owner_ref[axis] = out[:, :items]


def relax(table, returned, field, cols, n_ty, n_tx):
    f32 = jnp.float32
    rows = field.shape[0]
    dma = pltpu.SemaphoreType.DMA
    return pl.pallas_call(
        functools.partial(relax_kernel, n_ty, n_tx),
        out_shape=[
            jax.ShapeDtypeStruct((2, 1, table.shape[1]), f32),
            jax.ShapeDtypeStruct((2, rows, cols), f32),
        ],
        in_specs=[SMEM, VMEM, VMEM],
        out_specs=[VMEM, VMEM],
        scratch_shapes=[
            pltpu.VMEM(returned.shape, f32),
            pltpu.VMEM((3, rows + 16, LANES), f32),
            dma((n_tx,)),
            dma((n_tx,)),
            dma((8,)),
            dma((8,)),
        ],
        compiler_params=pltpu.CompilerParams(
            collective_id=1, has_side_effects=True, vmem_limit_bytes=8 * 2**20
        ),
        name="relax",
    )(table, returned, field)


def cut_kernel(items, table_ref, a_ref, out_ref, wide):
    rows, cols = a_ref.shape
    for part in range(cols // LANES):
        wide[part] = a_ref[:, part * LANES : (part + 1) * LANES].astype(jnp.float32)
    wide[cols // LANES] = jnp.zeros((rows, LANES), jnp.float32)

    def one(j, carry):
        top = table_ref[0, j]
        left = table_ref[1, j]
        base = left // LANES
        block = jnp.concatenate([wide[base + p, pl.ds(top, PATCH), :] for p in range(2)], axis=1)
        block = pltpu.roll(block, (2 * LANES - left % LANES) % (2 * LANES), 1)
        out_ref[table_ref[2, j]] = block[:, :PATCH].astype(jnp.bfloat16)
        return carry

    lax.fori_loop(0, items, one, 0)


def cut_templates(section_a, table, slots):
    rows, cols = section_a.shape
    return pl.pallas_call(
        functools.partial(cut_kernel, table.shape[1]),
        out_shape=jax.ShapeDtypeStruct((slots, PATCH, PATCH), jnp.bfloat16),
        in_specs=[SMEM, VMEM],
        out_specs=VMEM,
        scratch_shapes=[pltpu.VMEM((cols // LANES + 1, rows, LANES), jnp.float32)],
        compiler_params=pltpu.CompilerParams(vmem_limit_bytes=24 * 2**20),
        name="cut",
    )(table, section_a)


def flow_kernel(
    items,
    left_pad,
    tile,
    table_ref,
    b_ref,
    t_ref,
    mask_ref,
    ret_ref,
    field_ref,
    source_ref,
    wide,
    win,
    shifted,
    temp,
    corrs,
    scales,
):
    f32 = jnp.float32
    rows_b, cols_b = b_ref.shape
    for part in range(wide.shape[0]):
        held = max(0, min(LANES, cols_b - part * LANES))
        if held < LANES:
            wide[part] = jnp.zeros((rows_b, LANES), f32)
        if held:
            wide[part, :, :held] = b_ref[:, part * LANES : part * LANES + held].astype(f32)
    win[:, WIN:, :] = jnp.zeros((items, win.shape[1] - WIN, 2 * LANES), f32)
    lane = lax.broadcasted_iota(jnp.int32, (64, LANES), 1)
    shift = lax.broadcasted_iota(jnp.int32, (64, LANES), 0)
    low = (lane >= shift).astype(f32).astype(jnp.bfloat16)
    high = (lane < shift).astype(f32).astype(jnp.bfloat16)
    row_of = lax.broadcasted_iota(jnp.int32, (8, 2 * LANES), 0)
    win_lane = lax.broadcasted_iota(jnp.int32, (WIN, 2 * LANES), 1)

    def one(m, carry):
        top = table_ref[3, m]
        left = table_ref[4, m] + left_pad
        base = left // LANES
        block = jnp.concatenate([wide[base + p, pl.ds(top, WIN), :] for p in range(3)], axis=1)
        block = pltpu.roll(block, (3 * LANES - left % LANES) % (3 * LANES), 1)
        window = jnp.where(win_lane < WIN, block[:, : 2 * LANES], 0.0)
        win[m, :WIN, :] = window
        template = t_ref[table_ref[5, m]]
        temp[m] = template.astype(f32)
        for s in range(16 // GROUP):
            shifted[m, s] = win[m, pl.ds(s * GROUP, shifted.shape[2]), :].astype(jnp.bfloat16)
        temp_f = temp[m]
        energy_t = jnp.sum(temp_f * temp_f, keepdims=True) / (PATCH * PATCH)
        energy_w = jnp.sum(window * window, keepdims=True) / (WIN * WIN)
        scales[m] = jnp.broadcast_to((energy_t + EPSILON) * (energy_w + EPSILON), (8, LANES))

        def rows16(step, total):
            row0 = pl.multiple_of(step * 16, 16)
            sixteen = temp[m, pl.ds(row0, 16), :]
            placed, moved = [], []
            for s in range(16 // GROUP):
                parts = []
                for g in range(GROUP):
                    row = jnp.broadcast_to(
                        sixteen[s * GROUP + g : s * GROUP + g + 1, :], (64, LANES)
                    )
                    turned = pltpu.roll(row, 0, 1, stride=1, stride_axis=0)
                    turned = turned.astype(jnp.bfloat16)
                    parts.append(jnp.concatenate([turned * low, turned * high], axis=1))
                placed.append(jnp.concatenate(parts, axis=0))
                moved.append(shifted[m, s, pl.ds(row0, SPAN), :])
            return total + lax.dot_general(
                jnp.concatenate(placed, axis=1),
                jnp.concatenate(moved, axis=1),
                (((1,), (1,)), ((), ())),
                preferred_element_type=f32,
            )

        total = lax.fori_loop(
            0, PATCH // 16, rows16, jnp.zeros((GROUP * 64, SPAN), f32), unroll=True
        )
        corr = total[:64]
        for g in range(1, GROUP):
            corr = corr + pltpu.roll(total[g * 64 : g * 64 + 64], SPAN - g, 1)
        corrs[m, :64, :] = corr
        far = pltpu.roll(window, 2 * LANES - 64, 1)[:, :LANES].astype(jnp.bfloat16)
        far = jnp.concatenate([far, jnp.zeros((2 * LANES - WIN, LANES), jnp.bfloat16)], axis=0)
        cross = lax.dot_general(
            template, far, (((1,), (1,)), ((), ())), preferred_element_type=f32
        )
        moved = cross[:8]
        for q in range(1, PATCH // 8):
            moved = moved + pltpu.roll(cross[8 * q : 8 * q + 8], 2 * LANES - 8 * q, 1)
        for bit in (1, 2, 4):
            moved = jnp.where(row_of & bit != 0, pltpu.roll(moved, 2 * LANES - bit, 1), moved)
        last = jnp.sum(moved, axis=0, keepdims=True)
        corrs[m, 64:72, :] = jnp.broadcast_to(last[:, :LANES], (8, LANES))
        return carry

    lax.fori_loop(0, items, one, 0, unroll=4)

    corr = corrs[...]
    scale = SHARPNESS / (PATCH * PATCH * jnp.sqrt(scales[...]))
    dx = lax.broadcasted_iota(jnp.int32, corr.shape, 1)
    dy = lax.broadcasted_iota(jnp.int32, corr.shape, 2)
    inside = (dy < SHIFTS) & (dx < SHIFTS)
    scores = jnp.where(inside, corr * scale[:, 0:1, :], jnp.finfo(f32).min)
    peak = jnp.max(jnp.max(scores, axis=1, keepdims=True), axis=2, keepdims=True)
    weights = jnp.where(inside, jnp.exp(scores - peak), 0.0)
    by_col = jnp.sum(weights, axis=1, keepdims=True)
    norm = jnp.sum(by_col, axis=2, keepdims=True)
    dy_of = (dy[:, 0:1, :] - RADIUS).astype(f32)
    flow_y = jnp.sum(by_col * dy_of, axis=2, keepdims=True) / norm / FLOW_UNIT
    by_dx = jnp.sum(weights * (dx - RADIUS).astype(f32), axis=1, keepdims=True)
    flow_x = jnp.sum(by_dx, axis=2, keepdims=True) / norm / FLOW_UNIT
    flow_y = jnp.broadcast_to(flow_y, (items, 1, LANES))
    flow_x = jnp.broadcast_to(flow_x, (items, 1, LANES))
    node_rows, node_cols = mask_ref.shape
    at_row = lax.broadcasted_iota(jnp.int32, (node_rows, LANES), 0)
    at_col = lax.broadcasted_iota(jnp.int32, (node_rows, LANES), 1)
    field = jnp.zeros((node_rows, LANES), f32)
    out_lane = lax.broadcasted_iota(jnp.int32, (1, LANES), 1)
    out_y = jnp.zeros((1, LANES), f32)
    out_x = jnp.zeros((1, LANES), f32)
    for m in range(items):
        slot = table_ref[5, m]
        ret_ref[slot // CAP, pl.ds(slot % CAP * 2, 1), :] = flow_y[m]
        ret_ref[slot // CAP, pl.ds(slot % CAP * 2 + 1, 1), :] = flow_x[m]
        centre_y = (table_ref[3, m] + PATCH // 2) * node_rows // tile
        centre_x = (table_ref[4, m] + PATCH // 2) * node_cols // tile
        here = at_row == centre_y
        for part, value in ((1, -flow_y[m]), (2, -flow_x[m]), (3, 1.0)):
            at = at_col == centre_x + part * node_cols
            field = field + jnp.where(here & at, value, 0.0)
        out_y = jnp.where(out_lane == m, -flow_y[m], out_y)
        out_x = jnp.where(out_lane == m, -flow_x[m], out_x)
    field_ref[...] = field
    field_ref[:, :node_cols] = mask_ref[...].astype(f32)
    source_ref[0] = out_y[:, :items]
    source_ref[1] = out_x[:, :items]


def pair_flows(wide_b, arrived, table, node_mask, left_pad, tile, devices):
    items = table.shape[1]
    rows_b = wide_b.shape[0]
    node_rows = node_mask.shape[0]
    f32 = jnp.float32
    cols_w = max(wide_b.shape[1], (tile - PATCH + left_pad) // LANES * LANES + 3 * LANES)
    cols_w = (cols_w + LANES - 1) // LANES * LANES
    return pl.pallas_call(
        functools.partial(flow_kernel, items, left_pad, tile),
        out_shape=[
            jax.ShapeDtypeStruct((devices, 8, LANES), f32),
            jax.ShapeDtypeStruct((node_rows, LANES), f32),
            jax.ShapeDtypeStruct((2, 1, items), f32),
        ],
        in_specs=[SMEM, VMEM, VMEM, VMEM],
        out_specs=[VMEM, VMEM, VMEM],
        scratch_shapes=[
            pltpu.VMEM((cols_w // LANES, rows_b, LANES), f32),
            pltpu.VMEM((items, WIN + 80, 2 * LANES), f32),
            pltpu.VMEM((items, 16 // GROUP, WIN + 64, 2 * LANES), jnp.bfloat16),
            pltpu.VMEM((items, PATCH, LANES), f32),
            pltpu.VMEM((items, 72, LANES), f32),
            pltpu.VMEM((items, 8, LANES), f32),
        ],
        compiler_params=pltpu.CompilerParams(vmem_limit_bytes=32 * 2**20),
        name="pair_flows",
    )(table, wide_b, arrived, node_mask)


def shards(
    section_a, section_b, template_corner, template_slot, window_corner, window_slot, node_mask
):
    tile = section_a.shape[0]
    n_ty, n_tx = lax.axis_size("ty"), lax.axis_size("tx")
    table = jnp.concatenate(
        [template_corner[:, 0], template_slot, window_corner[:, 0], window_slot], axis=0
    )
    outgoing = cut_templates(section_a, table, n_tx * CAP)
    b_wide, arrived = gather(section_b, outgoing, n_ty, n_tx)
    returned, field, source_flow = pair_flows(
        b_wide, arrived, table, node_mask, LANES - RADIUS, tile, n_tx
    )
    owner_flow, displace = relax(
        table, returned, field, node_mask.shape[1], n_ty, n_tx
    )
    return (owner_flow, source_flow, displace)


def solution(mesh):
    placed = (
        P("ty", "tx"),
        P("ty", "tx"),
        P(None, "ty", "tx"),
        P("ty", "tx"),
        P(None, "ty", "tx"),
        P("ty", "tx"),
        P("ty", "tx"),
    )
    return jax.shard_map(
        shards,
        mesh=mesh,
        in_specs=placed,
        out_specs=(P(None, "ty", "tx"), P(None, "ty", "tx"), P(None, "ty", "tx")),
        check_vma=False,
    )
```

```python
import functools

import jax
import jax.numpy as jnp
from jax import lax
from jax.experimental import pallas as pl
from jax.experimental.pallas import tpu as pltpu
from jax.sharding import PartitionSpec as P

PATCH = 128
SHIFTS = 65
RADIUS = 32
WIN = 192
CAP = 2
ITERS_R = 3
LANES = 128
GROUP = 4
SPAN = 128


SHARPNESS = 256.0
SPRING_RATE = 0.25
FLOW_RATE = 0.5
FLOW_UNIT = 8.0
EPSILON = 1e-05
VMEM = pl.BlockSpec(memory_space=pltpu.VMEM)
SMEM = pl.BlockSpec(memory_space=pltpu.SMEM)
ANY = pl.BlockSpec(memory_space=pl.ANY)


DIRECTIONS = tuple((r, c) for r in (-1, 0, 1) for c in (-1, 0, 1) if (r, c) != (0, 0))
MESH = pl.DeviceIdType.MESH


def within(n_ty, n_tx, row, col):
    return (row >= 0) & (row < n_ty) & (col >= 0) & (col < n_tx)


def greet(n_ty, n_tx):
    ty, tx = lax.axis_index("ty"), lax.axis_index("tx")
    barrier = pltpu.get_barrier_semaphore()
    waits = n_tx - 1
    for step in range(1, n_tx):
        pl.semaphore_signal(
            barrier, inc=1, device_id=(ty, lax.rem(tx + step, n_tx)), device_id_type=MESH
        )
    for r, c in DIRECTIONS:
        if r == 0:
            continue
        there = within(n_ty, n_tx, ty + r, tx + c)

        @pl.when(there)
        def _():
            pl.semaphore_signal(barrier, inc=1, device_id=(ty + r, tx + c), device_id_type=MESH)

        waits = waits + there.astype(jnp.int32)
    pl.semaphore_wait(barrier, waits)


def to_row(n_tx, source, landing, width, send, recv):
    ty, tx = lax.axis_index("ty"), lax.axis_index("tx")
    copies = []
    for step in range(1, n_tx):
        peer = lax.rem(tx + step, n_tx)
        copies.append(
            pltpu.make_async_remote_copy(
                src_ref=source.at[pl.ds(peer * width, width)],
                dst_ref=landing.at[pl.ds(tx * width, width)],
                send_sem=send.at[step],
                recv_sem=recv.at[step],
                device_id=(ty, peer),
                device_id_type=MESH,
            )
        )
    return copies


def edges_of(step, size, rim, pad):
    if step == 0:
        return pl.ds(0, size), pl.ds(pad, size)
    if step < 0:
        return pl.ds(0, rim), pl.ds(pad + size, rim)
    return pl.ds(size - rim, rim), pl.ds(pad - rim, rim)


def gather_kernel(n_ty, n_tx, b_ref, out_ref, rim_ref, wide, landed, sides, zeros, send, recv, hsend, hrecv, own):
    ty, tx = lax.axis_index("ty"), lax.axis_index("tx")
    rows, cols = b_ref.shape
    zeros[...] = jnp.zeros(zeros.shape, zeros.dtype)
    tile_copy = pltpu.make_async_copy(
        b_ref, wide.at[pl.ds(RADIUS, rows), pl.ds(LANES, cols)], own.at[8]
    )
    tile_copy.start()
    mine = pl.ds(tx * CAP, CAP)
    own_copy = pltpu.make_async_copy(out_ref.at[mine], landed.at[mine], own.at[9])
    own_copy.start()
    greet(n_ty, n_tx)
    copies = to_row(n_tx, out_ref, landed, CAP, send, recv)
    for copy in copies:
        copy.start()
    rims = []
    for d, (r, c) in enumerate(DIRECTIONS):
        row_from, row_to = edges_of(r, rows, RADIUS, RADIUS)
        col_from, col_to = edges_of(c, cols, LANES, LANES)
        from_ref, to_ref = b_ref.at[row_from, col_from], wide.at[row_to, col_to]
        high, broad = row_to.size, col_to.size
        if r == 0:
            side = (1 + c) // 2
            from_ref, to_ref = rim_ref.at[side], sides.at[side]
            high, broad = rim_ref.shape[1], LANES
        rim = pltpu.make_async_remote_copy(
            src_ref=from_ref,
            dst_ref=to_ref,
            send_sem=hsend.at[d],
            recv_sem=hrecv.at[d],
            device_id=(ty + r, tx + c),
            device_id_type=MESH,
        )
        fill = pltpu.make_async_copy(
            zeros.at[pl.ds(0, high), pl.ds(0, broad)],
            to_ref,
            own.at[d],
        )
        goes = within(n_ty, n_tx, ty + r, tx + c)
        comes = within(n_ty, n_tx, ty - r, tx - c)
        pl.when(goes)(rim.start)
        pl.when(jnp.logical_not(comes))(fill.start)
        rims.append((goes, comes, rim, fill))
    for goes, comes, rim, fill in rims:
        pl.when(comes)(rim.wait_recv)
        pl.when(jnp.logical_not(comes))(fill.wait)
        pl.when(goes)(rim.wait_send)
    tile_copy.wait()
    own_copy.wait()
    for copy in copies:
        copy.wait()


def gather(section_b, outgoing, edges, n_ty, n_tx):
    rows, cols = section_b.shape
    dma = pltpu.SemaphoreType.DMA
    return pl.pallas_call(
        functools.partial(gather_kernel, n_ty, n_tx),
        out_shape=[
            jax.ShapeDtypeStruct((rows + 2 * RADIUS, cols + 2 * LANES), jnp.bfloat16),
            jax.ShapeDtypeStruct(outgoing.shape, jnp.bfloat16),
            jax.ShapeDtypeStruct(edges.shape, jnp.bfloat16),
        ],
        in_specs=[ANY, ANY, ANY],
        out_specs=[ANY, ANY, ANY],
        scratch_shapes=[
            pltpu.VMEM((rows, cols), jnp.bfloat16),
            dma((n_tx,)),
            dma((n_tx,)),
            dma((8,)),
            dma((8,)),
            dma((10,)),
        ],
        compiler_params=pltpu.CompilerParams(
            collective_id=0, has_side_effects=True, vmem_limit_bytes=8 * 2**20
        ),
        name="gather",
    )(section_b, outgoing, edges)


def relax_kernel(
    n_ty, n_tx, table_ref, ret_ref, field_ref, owner_ref, moved_ref, landed, ext, send, recv, hsend, hrecv
):
    f32 = jnp.float32
    ty, tx = lax.axis_index("ty"), lax.axis_index("tx")
    rows = field_ref.shape[0]
    cols = moved_ref.shape[2]
    items = owner_ref.shape[2]
    greet(n_ty, n_tx)
    copies = to_row(n_tx, ret_ref, landed, 1, send, recv)
    rims = []
    for d, (r, c) in enumerate(DIRECTIONS):
        row_from, row_to = edges_of(r, rows, 8, 8)
        rim = pltpu.make_async_remote_copy(
            src_ref=field_ref.at[row_from],
            dst_ref=ext.at[1 - c, row_to],
            send_sem=hsend.at[d],
            recv_sem=hrecv.at[d],
            device_id=(ty + r, tx + c),
            device_id_type=MESH,
        )
        goes = within(n_ty, n_tx, ty + r, tx + c)
        comes = within(n_ty, n_tx, ty - r, tx - c)
        pl.when(goes)(rim.start)
        rims.append((goes, comes, rim, 1 - c, row_to))
    for copy in copies:
        copy.start()
    landed[pl.ds(tx, 1)] = ret_ref[pl.ds(tx, 1)]
    ext[1, 8 : 8 + rows, :] = field_ref[...]
    for goes, comes, rim, side, row_to in rims:

        @pl.when(jnp.logical_not(comes))
        def _():
            ext[side, row_to, :] = jnp.zeros((row_to.size, LANES), f32)

    for goes, comes, rim, side, row_to in rims:
        pl.when(comes)(rim.wait_recv)
    lane = lax.broadcasted_iota(jnp.int32, (rows + 16, LANES), 1)
    left, middle, right = ext[0], ext[1], ext[2]

    def spread(field):
        at = field * cols
        wide = jnp.where(lane < 8 + cols, pltpu.roll(middle, (8 - at) % LANES, 1), 0.0)
        wide = jnp.where(lane < 8, pltpu.roll(left, (8 - at - cols) % LANES, 1), wide)
        beyond = (lane >= 8 + cols) & (lane < 16 + cols)
        return jnp.where(beyond, pltpu.roll(right, (8 + cols - at) % LANES, 1), wide)

    def around(grid):
        return (
            pltpu.roll(grid, 1, 0),
            pltpu.roll(grid, rows + 15, 0),
            pltpu.roll(grid, 1, 1),
            pltpu.roll(grid, LANES - 1, 1),
        )

    mask, count = spread(0), spread(3)
    pairs = [mask * near for near in around(mask)]
    for axis in range(2):
        target = spread(1 + axis)
        displace = jnp.zeros((rows + 16, LANES), f32)
        for sweep in range(ITERS_R):
            spring = jnp.zeros((rows + 16, LANES), f32)
            for pair, near in zip(pairs, around(displace)):
                spring = spring + pair * (near - displace)
            displace = (
                displace + SPRING_RATE * spring + FLOW_RATE * (target - count * displace)
            )
        moved_ref[axis] = pltpu.roll(displace, LANES - 8, 1)[8 : 8 + rows, :cols]
    for copy in copies:
        copy.wait()
    for goes, comes, rim, side, row_to in rims:
        pl.when(goes)(rim.wait_send)
    out_lane = lax.broadcasted_iota(jnp.int32, (1, LANES), 1)
    for axis in range(2):
        out = jnp.zeros((1, LANES), f32)
        for j in range(items):
            slot = table_ref[2, j]
            value = landed[slot // CAP, pl.ds(slot % CAP * 2 + axis, 1), :]
            out = jnp.where(out_lane == j, value, out)
        owner_ref[axis] = out[:, :items]


def relax(table, returned, field, cols, n_ty, n_tx):
    f32 = jnp.float32
    rows = field.shape[0]
    dma = pltpu.SemaphoreType.DMA
    return pl.pallas_call(
        functools.partial(relax_kernel, n_ty, n_tx),
        out_shape=[
            jax.ShapeDtypeStruct((2, 1, table.shape[1]), f32),
            jax.ShapeDtypeStruct((2, rows, cols), f32),
        ],
        in_specs=[SMEM, VMEM, VMEM],
        out_specs=[VMEM, VMEM],
        scratch_shapes=[
            pltpu.VMEM(returned.shape, f32),
            pltpu.VMEM((3, rows + 16, LANES), f32),
            dma((n_tx,)),
            dma((n_tx,)),
            dma((8,)),
            dma((8,)),
        ],
        compiler_params=pltpu.CompilerParams(
            collective_id=1, has_side_effects=True, vmem_limit_bytes=8 * 2**20
        ),
        name="relax",
    )(table, returned, field)


def cut_kernel(items, table_ref, a_ref, b_ref, out_ref, rim_ref, wide):
    rows, cols = a_ref.shape
    for part in range(cols // LANES):
        wide[part] = a_ref[:, part * LANES : (part + 1) * LANES].astype(jnp.float32)
    wide[cols // LANES] = jnp.zeros((rows, LANES), jnp.float32)

    depth = rim_ref.shape[1]
    at = lax.broadcasted_iota(jnp.int32, (depth, LANES), 1) // RADIUS
    for side in range(2):
        base = side * (cols - LANES)
        packed = jnp.zeros((depth, LANES), jnp.float32)
        for q in range(LANES // RADIUS):
            block = b_ref[q * depth : (q + 1) * depth, base : base + LANES].astype(jnp.float32)
            turn = (q * RADIUS - side * (LANES - RADIUS)) % LANES
            packed = jnp.where(at == q, pltpu.roll(block, turn, 1), packed)
        rim_ref[side] = packed.astype(jnp.bfloat16)

    def one(j, carry):
        top = table_ref[0, j]
        left = table_ref[1, j]
        base = left // LANES
        block = jnp.concatenate([wide[base + p, pl.ds(top, PATCH), :] for p in range(2)], axis=1)
        block = pltpu.roll(block, (2 * LANES - left % LANES) % (2 * LANES), 1)
        out_ref[table_ref[2, j]] = block[:, :PATCH].astype(jnp.bfloat16)
        return carry

    lax.fori_loop(0, items, one, 0)


def cut_templates(section_a, section_b, table, slots):
    rows, cols = section_a.shape
    return pl.pallas_call(
        functools.partial(cut_kernel, table.shape[1]),
        out_shape=[
            jax.ShapeDtypeStruct((slots, PATCH, PATCH), jnp.bfloat16),
            jax.ShapeDtypeStruct((2, rows * RADIUS // LANES, LANES), jnp.bfloat16),
        ],
        in_specs=[SMEM, VMEM, VMEM],
        out_specs=[VMEM, VMEM],
        scratch_shapes=[pltpu.VMEM((cols // LANES + 1, rows, LANES), jnp.float32)],
        compiler_params=pltpu.CompilerParams(vmem_limit_bytes=24 * 2**20),
        name="cut",
    )(table, section_a, section_b)


def flow_kernel(
    items,
    left_pad,
    tile,
    table_ref,
    b_ref,
    t_ref,
    side_ref,
    mask_ref,
    ret_ref,
    field_ref,
    source_ref,
    wide,
    win,
    shifted,
    temp,
    corrs,
    scales,
):
    f32 = jnp.float32
    rows_b, cols_b = b_ref.shape
    for part in range(wide.shape[0]):
        held = max(0, min(LANES, cols_b - part * LANES))
        if held < LANES:
            wide[part] = jnp.zeros((rows_b, LANES), f32)
        if held:
            wide[part, :, :held] = b_ref[:, part * LANES : part * LANES + held].astype(f32)
    depth = side_ref.shape[1]
    for side, part in ((0, cols_b // LANES - 1), (1, 0)):
        packed = side_ref[side].astype(f32)
        for q in range(LANES // RADIUS):
            turn = (side * (LANES - RADIUS) - q * RADIUS) % LANES
            row0 = RADIUS + q * depth
            wide[part, row0 : row0 + depth, :] = pltpu.roll(packed, turn, 1)
    win[:, WIN:, :] = jnp.zeros((items, win.shape[1] - WIN, 2 * LANES), f32)
    lane = lax.broadcasted_iota(jnp.int32, (64, LANES), 1)
    shift = lax.broadcasted_iota(jnp.int32, (64, LANES), 0)
    low = (lane >= shift).astype(f32).astype(jnp.bfloat16)
    high = (lane < shift).astype(f32).astype(jnp.bfloat16)
    row_of = lax.broadcasted_iota(jnp.int32, (8, 2 * LANES), 0)
    win_lane = lax.broadcasted_iota(jnp.int32, (WIN, 2 * LANES), 1)

    def one(m, carry):
        top = table_ref[3, m]
        left = table_ref[4, m] + left_pad
        base = left // LANES
        block = jnp.concatenate([wide[base + p, pl.ds(top, WIN), :] for p in range(3)], axis=1)
        block = pltpu.roll(block, (3 * LANES - left % LANES) % (3 * LANES), 1)
        window = jnp.where(win_lane < WIN, block[:, : 2 * LANES], 0.0)
        win[m, :WIN, :] = window
        template = t_ref[table_ref[5, m]]
        temp[m] = template.astype(f32)
        for s in range(16 // GROUP):
            shifted[m, s] = win[m, pl.ds(s * GROUP, shifted.shape[2]), :].astype(jnp.bfloat16)
        temp_f = temp[m]
        energy_t = jnp.sum(temp_f * temp_f, keepdims=True) / (PATCH * PATCH)
        energy_w = jnp.sum(window * window, keepdims=True) / (WIN * WIN)
        scales[m] = jnp.broadcast_to((energy_t + EPSILON) * (energy_w + EPSILON), (8, LANES))

        def rows16(step, total):
            row0 = pl.multiple_of(step * 16, 16)
            sixteen = temp[m, pl.ds(row0, 16), :]
            placed, moved = [], []
            for s in range(16 // GROUP):
                parts = []
                for g in range(GROUP):
                    row = jnp.broadcast_to(
                        sixteen[s * GROUP + g : s * GROUP + g + 1, :], (64, LANES)
                    )
                    turned = pltpu.roll(row, 0, 1, stride=1, stride_axis=0)
                    turned = turned.astype(jnp.bfloat16)
                    parts.append(jnp.concatenate([turned * low, turned * high], axis=1))
                placed.append(jnp.concatenate(parts, axis=0))
                moved.append(shifted[m, s, pl.ds(row0, SPAN), :])
            return total + lax.dot_general(
                jnp.concatenate(placed, axis=1),
                jnp.concatenate(moved, axis=1),
                (((1,), (1,)), ((), ())),
                preferred_element_type=f32,
            )

        total = lax.fori_loop(
            0, PATCH // 16, rows16, jnp.zeros((GROUP * 64, SPAN), f32), unroll=True
        )
        corr = total[:64]
        for g in range(1, GROUP):
            corr = corr + pltpu.roll(total[g * 64 : g * 64 + 64], SPAN - g, 1)
        corrs[m, :64, :] = corr
        far = pltpu.roll(window, 2 * LANES - 64, 1)[:, :LANES].astype(jnp.bfloat16)
        far = jnp.concatenate([far, jnp.zeros((2 * LANES - WIN, LANES), jnp.bfloat16)], axis=0)
        cross = lax.dot_general(
            template, far, (((1,), (1,)), ((), ())), preferred_element_type=f32
        )
        moved = cross[:8]
        for q in range(1, PATCH // 8):
            moved = moved + pltpu.roll(cross[8 * q : 8 * q + 8], 2 * LANES - 8 * q, 1)
        for bit in (1, 2, 4):
            moved = jnp.where(row_of & bit != 0, pltpu.roll(moved, 2 * LANES - bit, 1), moved)
        last = jnp.sum(moved, axis=0, keepdims=True)
        corrs[m, 64:72, :] = jnp.broadcast_to(last[:, :LANES], (8, LANES))
        return carry

    lax.fori_loop(0, items, one, 0, unroll=4)

    corr = corrs[...]
    scale = SHARPNESS / (PATCH * PATCH * jnp.sqrt(scales[...]))
    dx = lax.broadcasted_iota(jnp.int32, corr.shape, 1)
    dy = lax.broadcasted_iota(jnp.int32, corr.shape, 2)
    inside = (dy < SHIFTS) & (dx < SHIFTS)
    scores = jnp.where(inside, corr * scale[:, 0:1, :], jnp.finfo(f32).min)
    peak = jnp.max(jnp.max(scores, axis=1, keepdims=True), axis=2, keepdims=True)
    weights = jnp.where(inside, jnp.exp(scores - peak), 0.0)
    by_col = jnp.sum(weights, axis=1, keepdims=True)
    norm = jnp.sum(by_col, axis=2, keepdims=True)
    dy_of = (dy[:, 0:1, :] - RADIUS).astype(f32)
    flow_y = jnp.sum(by_col * dy_of, axis=2, keepdims=True) / norm / FLOW_UNIT
    by_dx = jnp.sum(weights * (dx - RADIUS).astype(f32), axis=1, keepdims=True)
    flow_x = jnp.sum(by_dx, axis=2, keepdims=True) / norm / FLOW_UNIT
    flow_y = jnp.broadcast_to(flow_y, (items, 1, LANES))
    flow_x = jnp.broadcast_to(flow_x, (items, 1, LANES))
    node_rows, node_cols = mask_ref.shape
    at_row = lax.broadcasted_iota(jnp.int32, (node_rows, LANES), 0)
    at_col = lax.broadcasted_iota(jnp.int32, (node_rows, LANES), 1)
    field = jnp.zeros((node_rows, LANES), f32)
    out_lane = lax.broadcasted_iota(jnp.int32, (1, LANES), 1)
    out_y = jnp.zeros((1, LANES), f32)
    out_x = jnp.zeros((1, LANES), f32)
    for m in range(items):
        slot = table_ref[5, m]
        ret_ref[slot // CAP, pl.ds(slot % CAP * 2, 1), :] = flow_y[m]
        ret_ref[slot // CAP, pl.ds(slot % CAP * 2 + 1, 1), :] = flow_x[m]
        centre_y = (table_ref[3, m] + PATCH // 2) * node_rows // tile
        centre_x = (table_ref[4, m] + PATCH // 2) * node_cols // tile
        here = at_row == centre_y
        for part, value in ((1, -flow_y[m]), (2, -flow_x[m]), (3, 1.0)):
            at = at_col == centre_x + part * node_cols
            field = field + jnp.where(here & at, value, 0.0)
        out_y = jnp.where(out_lane == m, -flow_y[m], out_y)
        out_x = jnp.where(out_lane == m, -flow_x[m], out_x)
    field_ref[...] = field
    field_ref[:, :node_cols] = mask_ref[...].astype(f32)
    source_ref[0] = out_y[:, :items]
    source_ref[1] = out_x[:, :items]


def pair_flows(wide_b, arrived, sides, table, node_mask, left_pad, tile, devices):
    items = table.shape[1]
    rows_b = wide_b.shape[0]
    node_rows = node_mask.shape[0]
    f32 = jnp.float32
    cols_w = max(wide_b.shape[1], (tile - PATCH + left_pad) // LANES * LANES + 3 * LANES)
    cols_w = (cols_w + LANES - 1) // LANES * LANES
    return pl.pallas_call(
        functools.partial(flow_kernel, items, left_pad, tile),
        out_shape=[
            jax.ShapeDtypeStruct((devices, 8, LANES), f32),
            jax.ShapeDtypeStruct((node_rows, LANES), f32),
            jax.ShapeDtypeStruct((2, 1, items), f32),
        ],
        in_specs=[SMEM, VMEM, VMEM, VMEM, VMEM],
        out_specs=[VMEM, VMEM, VMEM],
        scratch_shapes=[
            pltpu.VMEM((cols_w // LANES, rows_b, LANES), f32),
            pltpu.VMEM((items, WIN + 80, 2 * LANES), f32),
            pltpu.VMEM((items, 16 // GROUP, WIN + 64, 2 * LANES), jnp.bfloat16),
            pltpu.VMEM((items, PATCH, LANES), f32),
            pltpu.VMEM((items, 72, LANES), f32),
            pltpu.VMEM((items, 8, LANES), f32),
        ],
        compiler_params=pltpu.CompilerParams(vmem_limit_bytes=32 * 2**20),
        name="pair_flows",
    )(table, wide_b, arrived, sides, node_mask)


def shards(
    section_a, section_b, template_corner, template_slot, window_corner, window_slot, node_mask
):
    tile = section_a.shape[0]
    n_ty, n_tx = lax.axis_size("ty"), lax.axis_size("tx")
    table = jnp.concatenate(
        [template_corner[:, 0], template_slot, window_corner[:, 0], window_slot], axis=0
    )
    outgoing, edges = cut_templates(section_a, section_b, table, n_tx * CAP)
    b_wide, arrived, sides = gather(section_b, outgoing, edges, n_ty, n_tx)
    returned, field, source_flow = pair_flows(
        b_wide, arrived, sides, table, node_mask, LANES - RADIUS, tile, n_tx
    )
    owner_flow, displace = relax(
        table, returned, field, node_mask.shape[1], n_ty, n_tx
    )
    return (owner_flow, source_flow, displace)


def solution(mesh):
    placed = (
        P("ty", "tx"),
        P("ty", "tx"),
        P(None, "ty", "tx"),
        P("ty", "tx"),
        P(None, "ty", "tx"),
        P("ty", "tx"),
        P("ty", "tx"),
    )
    return jax.shard_map(
        shards,
        mesh=mesh,
        in_specs=placed,
        out_specs=(P(None, "ty", "tx"), P(None, "ty", "tx"), P(None, "ty", "tx")),
        check_vma=False,
    )
```
